512 devices in a mesh: tm: 32 (over x, y_hi, core), sku: 16 (over y_lo, z).
Axes of the slice: x: 4, y: 8 (y_hi: 4, y_lo: 2; y = y_hi * 2 + y_lo), z: 8, core: 2. Of those that a mesh axis runs over, the one named last changes fastest.
Arguments:
- primal_x: float32 [256, 131072], P('tm', 'sku'), may hold values from 0 to 2
- stock_v: float32 [256, 131072], P('tm', 'sku'), may hold values from 0 to 2
- balance_dual: float32 [256, 131072], P('tm', 'sku'), may hold values from -6 to 6
- plant_dual: float32 [256, 128], P('tm', 'sku'), may hold values from 0 to 1
- demand: float32 [256, 131072], P('tm', 'sku'), may hold values from 0.2 to 1.5
- unit_cost: float32 [131072], P('sku'), may hold values from 0.1 to 2
- holding_cost: float32 [131072], P('sku'), may hold values from 0.05 to 1
- load_coef: float32 [131072], P('sku'), may hold values from 0.25 to 2
- capacity: float32 [256, 128], P('tm'), may hold values from 307.2 to 1228.8
- lags: int32 [1024], P('sku'), may hold values from 1 to 8
- plants: int32 [131072], P('sku'), may hold values from 0 to 127
- step_codes: int32 [2], replicated, may hold values from 0 to 4
Outputs:
- next_x: float32 [256, 131072], P('tm', 'sku')
- next_v: float32 [256, 131072], P('tm', 'sku')
- next_balance: float32 [256, 131072], P('tm', 'sku')
- next_plant: float32 [256, 128], P('tm', 'sku')
- residuals: float32 [2, 2], replicated
The draws below stay inside these ranges and needn't reach their ends.
Inputs may be any that keep to these rules, and one draw needn't show every extreme that they name: `lags`: lead time of each block of 128 SKU-sites; 8 occurs.
All inputs are finite; a program needn't handle non-finite values.
Results may differ from the reference program's by a relative error of at most 0.0001.
Values sent between devices are 32-bit elements; how exact they have to be, the bound alone decides.
No kernel may reach another device: no remote copies, remote signals or barrier semaphores. Data moves between devices by JAX's collectives and lax.ppermute only.
A program may use at most 64 MiB of HBM per device.

```python
import math
import jax
import jax.numpy as jnp

P_SIZE = 128
LAGMAX = 8
BLOCK = 128
ITERS = 2
PERIODS = 256
SKUS = 131072


def with_ends(drawn, rng, smallest, high):
    longest = drawn.shape.index(max(drawn.shape))
    spots = []
    for shift in (0, 1):
        where = [jax.random.randint(jax.random.fold_in(rng, axis), (), 0, length) for axis, length in enumerate(drawn.shape)]
        where[longest] = (where[longest] + shift) % drawn.shape[longest]
        spots.append(tuple(where))
    return drawn.at[spots[0]].set(smallest).at[spots[1]].set(high)


def shard_levels(key, extent, pieces, low, top_value):
    factor_of = 1.0
    for axis_at, blocks in pieces:
        draws = jax.random.uniform(jax.random.fold_in(jax.random.fold_in(key, 6), axis_at), (blocks,), jnp.float32, low / len(pieces), top_value / len(pieces))
        factor_of = factor_of * jnp.repeat(jnp.exp(draws), extent[axis_at] // blocks).reshape((-1,) + (1,) * (len(extent) - 1 - axis_at))
    return factor_of


def gaussian(stream_key, dims, scale, bound, pieces=(), dtype=jnp.bfloat16):
    drawn = jax.random.normal(stream_key, dims, jnp.float32) * scale
    if len(pieces) > 0:
        drawn = shard_levels(stream_key, dims, pieces, -0.22, 0.18) * drawn
    return jnp.clip(drawn, min=-bound, max=bound).astype(dtype)


def setup_inputs(seed: int = 0) -> dict:
    key_list = jax.random.split(jax.random.key(seed), 13)
    primal_x = jnp.clip(2.0 * jax.random.uniform(key_list[0], (PERIODS, SKUS), jnp.float32) ** shard_levels(key_list[0], (PERIODS, SKUS), ((0, 32), (1, 16)), -0.2, 0.2), 0.0, 2.0)
    stock_v = jnp.clip(2.0 * jax.random.uniform(key_list[1], (PERIODS, SKUS), jnp.float32) ** shard_levels(key_list[1], (PERIODS, SKUS), ((0, 32), (1, 16)), -0.2, 0.2), 0.0, 2.0)
    balance_dual = gaussian(key_list[2], (PERIODS, SKUS), 1.0, 6.0, ((0, 32), (1, 16)), jnp.float32)
    plant_dual = jnp.clip(1.0 * jax.random.uniform(key_list[3], (PERIODS, P_SIZE), jnp.float32) ** shard_levels(key_list[3], (PERIODS, P_SIZE), ((0, 32), (1, 16)), -0.2, 0.2), 0.0, 1.0)
    demand = jnp.clip(0.2 + 1.3 * jax.random.uniform(key_list[4], (PERIODS, SKUS), jnp.float32) ** shard_levels(key_list[4], (PERIODS, SKUS), ((0, 32), (1, 16)), -0.2, 0.2), 0.2, 1.5)
    unit_cost = jnp.clip(jnp.exp(math.log(2.0) - 2.9957323 * jax.random.uniform(key_list[5], (SKUS,), jnp.float32) ** shard_levels(key_list[5], (SKUS,), ((0, 16),), -0.2, 0.2)), 0.1, 2.0)
    holding_cost = jnp.clip(jnp.exp(math.log(1.0) - 2.9957323 * jax.random.uniform(key_list[6], (SKUS,), jnp.float32) ** shard_levels(key_list[6], (SKUS,), ((0, 16),), -0.2, 0.2)), 0.05, 1.0)
    load_coef = jnp.clip(jnp.exp(math.log(2.0) - 2.0794415 * jax.random.uniform(key_list[7], (SKUS,), jnp.float32) ** shard_levels(key_list[7], (SKUS,), ((0, 16),), -0.2, 0.2)), 0.25, 2.0)
    capacity = jnp.clip(307.2 + 921.60004 * jax.random.uniform(key_list[8], (PERIODS, P_SIZE), jnp.float32) ** shard_levels(key_list[8], (PERIODS, P_SIZE), ((0, 32),), -0.2, 0.2), 307.2, 1228.8)
    lags = with_ends(jax.random.randint(key_list[9], (SKUS // BLOCK,), 1, LAGMAX + 1), jax.random.fold_in(key_list[9], 1), 1, LAGMAX).astype(jnp.int32)
    plants = with_ends(jax.random.randint(key_list[10], (SKUS,), 0, P_SIZE), jax.random.fold_in(key_list[10], 1), 0, P_SIZE - 1).astype(jnp.int32)
    step_codes = jax.random.randint(key_list[11], (2,), 0, 5).astype(jnp.int32)
    return dict(primal_x=primal_x, stock_v=stock_v, balance_dual=balance_dual, plant_dual=plant_dual, demand=demand, unit_cost=unit_cost, holding_cost=holding_cost, load_coef=load_coef, capacity=capacity, lags=lags, plants=plants, step_codes=step_codes)


def lagged_past(field, lag_cells):
    result = jnp.zeros_like(field)
    for offset in range(1, LAGMAX + 1):
        result = jnp.where(lag_cells == offset, jnp.roll(field, offset, axis=0), result)
    return result


def lagged_ahead(field, lag_cells):
    result = jnp.zeros_like(field)
    for offset in range(1, LAGMAX + 1):
        result = jnp.where(lag_cells == offset, jnp.roll(field, -offset, axis=0), result)
    return result


def reference(primal_x, stock_v, balance_dual, plant_dual, demand, unit_cost, holding_cost, load_coef, capacity, lags, plants, step_codes):
    primal_step = 0.05 * (step_codes[0].astype(jnp.float32) + 2.0)
    dual_step = 0.05 * (step_codes[1].astype(jnp.float32) + 2.0)
    plant_step = dual_step * (P_SIZE / SKUS)
    lag_cells = jnp.repeat(lags, BLOCK)[None, :]
    current_x = primal_x
    current_v = stock_v
    duals = balance_dual
    prices = plant_dual
    history = []
    for iteration in range(ITERS):
        ahead = lagged_ahead(duals, lag_cells)
        following = jnp.roll(duals, -1, axis=0)
        charged = prices[:, plants] * load_coef[None, :]
        new_x = jnp.maximum(current_x - primal_step * (unit_cost[None, :] + ahead + charged), 0.0)
        new_v = jnp.maximum(current_v - primal_step * (holding_cost[None, :] - duals + following), 0.0)
        bar_x = 2.0 * new_x - current_x
        bar_v = 2.0 * new_v - current_v
        misfit = -demand - (bar_v - jnp.roll(bar_v, 1, axis=0) - lagged_past(bar_x, lag_cells))
        duals = duals + dual_step * misfit
        loads = jax.ops.segment_sum((bar_x * load_coef[None, :]).T, plants, num_segments=P_SIZE).T
        excess = loads - capacity
        prices = jnp.maximum(prices + plant_step * excess, 0.0)
        violation = jnp.maximum(excess, 0.0) * (P_SIZE / SKUS)
        history.append(jnp.stack([jnp.mean(misfit * misfit), jnp.mean(violation * violation)]))
        current_x = new_x
        current_v = new_v
    return current_x, current_v, duals, prices, jnp.stack(history)
```

```python
import jax
import jax.numpy as jnp
from jax import lax
from jax.experimental import pallas as pl
from jax.experimental.pallas import tpu as pltpu
from jax.sharding import PartitionSpec as P

P_SIZE = 128
LAGMAX = 8
BLOCK = 128
ROWS = 8
F32 = jnp.float32
VMEM = pl.BlockSpec(memory_space=pltpu.VMEM)
SMEM = pl.BlockSpec(memory_space=pltpu.SMEM)


def shifted(value, axis, steps):
    count = lax.axis_size(axis)
    return lax.ppermute(value, axis, [(i, (i + steps) % count) for i in range(count)])


def spread(value, axis):
    return lax.all_to_all(value, axis, 0, 0, tiled=True)


def shape(*dims):
    return jax.ShapeDtypeStruct(dims, F32)


def call(kernel, out_shape, operands, smem=0, out_specs=None, scratch=(), name=None):
    size = sum(o.size * 4 for o in operands)
    outs = out_shape if isinstance(out_shape, tuple) else (out_shape,)
    size += sum(o.size * 4 for o in outs)
    return pl.pallas_call(
        kernel,
        out_shape=out_shape,
        in_specs=[SMEM] * smem + [VMEM] * (len(operands) - smem),
        out_specs=out_specs if out_specs is not None else jax.tree.map(lambda _: VMEM, out_shape),
        scratch_shapes=scratch,
        cost_estimate=pl.CostEstimate(flops=20 * size, bytes_accessed=size, transcendentals=0),
        name=name,
    )(*operands)


def step_size(codes, index):
    return 0.05 * (codes[index].astype(F32) + 2.0)


def row_ids():
    return lax.broadcasted_iota(jnp.int32, (ROWS, BLOCK), 0)


def wide(row):
    return jnp.broadcast_to(row, (ROWS, BLOCK))


def ahead(own, after, lag, rows):
    return pltpu.roll(jnp.where(rows >= lag, own, after), ROWS - lag, 0)


def past(own, before, lag, rows):
    return pltpu.roll(jnp.where(rows < ROWS - lag, own, before), lag & (ROWS - 1), 0)


def row_after(own, last, rows):
    return jnp.where(rows == ROWS - 1, last, pltpu.roll(own, ROWS - 1, 0))


def row_before(own, first, rows):
    return jnp.where(rows == 0, first, pltpu.roll(own, 1, 0))


def stock_step(stock, cost, dual, dual_after, primal):
    return jnp.maximum(stock - primal * (cost - dual + dual_after), 0.0)


def price_of(prices, plant_row):
    return jnp.take_along_axis(prices, wide(plant_row), axis=1, mode="promise_in_bounds")


def load_terms(values, plant_row, plant_ids):
    high = values.astype(jnp.bfloat16).astype(F32)
    rest = values - high
    middle = rest.astype(jnp.bfloat16).astype(F32)
    pieces = jnp.concatenate([high, middle, rest - middle], 0).astype(jnp.bfloat16)
    table = (plant_ids == plant_row).astype(F32).astype(jnp.bfloat16)
    return lax.dot_general(pieces, table, (((1,), (1,)), ((), ())), preferred_element_type=F32)


def folded(total):
    return total[0:8] + total[8:16] + total[16:24]


def blocks(width):
    return [(i, pl.ds(i * BLOCK, BLOCK)) for i in range(width // BLOCK)]


def first_kernel(codes, lags, gathered, x, y, y_next, cost, load, plants, x1, bar, loads, prices):
    primal = step_size(codes, 0)
    rows = row_ids()
    plant_ids = lax.broadcasted_iota(jnp.int32, (P_SIZE, BLOCK), 0)
    each = P_SIZE // gathered.shape[0]
    for j in range(gathered.shape[0]):
        prices[:, j * each : (j + 1) * each] = gathered[j, :, :each]
    w = prices[...]
    total = jnp.zeros((3 * ROWS, P_SIZE), F32)
    for i, at in blocks(x.shape[1]):
        dual = ahead(y[:, at], y_next[:, at], lags[i], rows)
        old = x[:, at]
        charged = price_of(w, plants[:, at]) * load[:, at]
        new = jnp.maximum(old - primal * (cost[:, at] + dual + charged), 0.0)
        over = 2.0 * new - old
        x1[:, at] = new
        bar[:, at] = over
        total += load_terms(over * load[:, at], plants[:, at], plant_ids)
    loads[...] = jnp.broadcast_to(folded(total)[None], loads.shape)


def middle_kernel(
    codes, lags, x, bar, bar_prev, bar_row, v, v_next, y, y_next, d, d_next, prev_rows, far_rows,
    holding, v2, y1, partial, edge, dual_x, field_x, squares,
):
    primal = step_size(codes, 0)
    dual_step = step_size(codes, 1)
    rows = row_ids()
    square = jnp.zeros((ROWS, BLOCK), F32)
    for i, at in blocks(x.shape[1]):
        lag = lags[i]
        cost = holding[:, at]
        ya, yb = y[:, at], y_next[:, at]
        va, vb = v[:, at], v_next[:, at]
        v_before, y_before = prev_rows[0:1, at], prev_rows[1:2, at]
        y16, y17 = far_rows[0:1, at], far_rows[1:2, at]
        v16, d16 = far_rows[2:3, at], far_rows[3:4, at]
        va1 = stock_step(va, cost, ya, row_after(ya, yb[0:1], rows), primal)
        vb1 = stock_step(vb, cost, yb, row_after(yb, y16, rows), primal)
        va_bar = 2.0 * va1 - va
        vb_bar = 2.0 * vb1 - vb
        before_bar = 2.0 * stock_step(v_before, cost, y_before, ya[0:1], primal) - v_before
        far_bar = 2.0 * stock_step(v16, cost, y16, y17, primal) - v16
        ha = -d[:, at] - va_bar + row_before(va_bar, before_bar, rows)
        hb = -d_next[:, at] - vb_bar + row_before(vb_bar, va_bar[7:8], rows)
        h16 = -d16 - far_bar + vb_bar[7:8]
        own = bar[:, at]
        shifted_misfit = ahead(ha, hb, lag, rows) + own
        square += shifted_misfit * shifted_misfit
        yx = ahead(ya, yb, lag, rows) + dual_step * shifted_misfit
        dual_x[:, at] = yx
        late = past(own, bar_prev[:, at], lag, rows)
        ya1 = ya + dual_step * (ha + late)
        y1[:, at] = ya1
        y8 = yb[0:1] + dual_step * (hb[0:1] + pltpu.roll(own, lag & (ROWS - 1), 0)[0:1])
        va2 = stock_step(va1, cost, ya1, row_after(ya1, y8, rows), primal)
        v2[:, at] = va2
        va2_bar = 2.0 * va2 - va1
        edge[:, at] = va2_bar[7:8]
        partial[:, at] = -d[:, at] - va2_bar + row_before(va2_bar, jnp.zeros((1, BLOCK), F32), rows)
        whole = lag == LAGMAX
        y_end = jnp.where(whole, y16, pltpu.roll(yb, ROWS - lag, 0)[0:1])
        h_end = jnp.where(whole, h16, pltpu.roll(hb, ROWS - lag, 0)[0:1])
        yx_end = y_end + dual_step * (h_end + bar_row[:, at])
        vx1 = ahead(va1, vb1, lag, rows)
        vx2 = stock_step(vx1, cost, yx, row_after(yx, yx_end, rows), primal)
        vx_bar = 2.0 * vx2 - vx1
        first = pltpu.roll(va2_bar, ROWS - lag + 1, 0)[0:1]
        dx = ahead(d[:, at], d_next[:, at], lag, rows)
        field_x[:, at] = -dx - vx_bar + row_before(vx_bar, first, rows)
    squares[...] = square


def second_kernel(
    codes, lags, sums, prices, cap, x, dual, field, squares, cost, load, plants,
    x2, bar, loads, prices_new, excess_row,
):
    primal = step_size(codes, 0)
    plant_step = step_size(codes, 1) * (P_SIZE / (x.shape[1] * sums.shape[0]))
    plant_ids = lax.broadcasted_iota(jnp.int32, (P_SIZE, BLOCK), 0)
    excess = jnp.sum(sums[...], axis=0) - cap[...]
    w = jnp.maximum(prices[...] + plant_step * excess, 0.0)
    prices_new[...] = w
    above = jnp.maximum(excess, 0.0)
    excess_row[...] = above * above
    total = jnp.zeros((3 * ROWS, P_SIZE), F32)
    square = jnp.zeros((ROWS, BLOCK), F32)
    for i, at in blocks(x.shape[1]):
        old = x[:, at]
        charged = price_of(w, plants[:, at]) * load[:, at]
        new = jnp.maximum(old - primal * (cost[:, at] + dual[:, at] + charged), 0.0)
        over = 2.0 * new - old
        x2[:, at] = new
        bar[:, at] = over
        misfit = field[:, at] + over
        square += misfit * misfit
        total += load_terms(over * load[:, at], plants[:, at], plant_ids)
    count = loads.shape[0]
    loads[:, 0:8, :] = jnp.broadcast_to(folded(total)[None], (count, ROWS, P_SIZE))
    loads[:, 8:16, :] = jnp.broadcast_to(squares[...][None], (count, ROWS, P_SIZE))
    loads[:, 16:24, :] = jnp.broadcast_to(square[None], (count, ROWS, P_SIZE))


def third_kernel(codes, sums, prices, cap, excess_row, price_out, out, *, total_skus):
    plant_step = step_size(codes, 1) * (P_SIZE / total_skus)
    totals = jnp.sum(sums[...], axis=0)
    excess = totals[0:8] - cap[...]
    price_out[...] = jnp.maximum(prices[...] + plant_step * excess, 0.0)
    above = jnp.maximum(excess, 0.0)
    parts = [totals[8:16], excess_row[...], totals[16:24], above * above]
    packed = jnp.concatenate([jnp.sum(p, axis=0, keepdims=True) for p in parts] * 2, 0)
    out[...] = jnp.broadcast_to(packed[None], out.shape)


def last_kernel(sums, out, *, cells, rows_all):
    scale = P_SIZE / (cells // (rows_all // P_SIZE))
    totals = jnp.sum(jnp.sum(sums[...], axis=0), axis=1, keepdims=True)
    for k in range(2):
        out[k, 0] = jnp.sum(totals[2 * k : 2 * k + 1]) / cells
        out[k, 1] = jnp.sum(totals[2 * k + 1 : 2 * k + 2]) * (scale * scale) / rows_all


def dual_kernel(codes, lags, y1, partial, edge, bar, bar_prev, out):
    dual_step = step_size(codes, 1)
    rows = row_ids()
    for i, at in blocks(y1.shape[1]):
        lag = lags[i]
        field = partial[:, at] + jnp.where(rows == 0, wide(edge[:, at]), 0.0)
        out[:, at] = y1[:, at] + dual_step * (field + past(bar[:, at], bar_prev[:, at], lag, rows))


def body(
    primal_x,
    stock_v,
    balance_dual,
    plant_dual,
    demand,
    unit_cost,
    holding_cost,
    load_coef,
    capacity,
    lags,
    plants,
    step_codes,
):
    width = primal_x.shape[1]
    skus = lax.axis_size("sku")
    times = lax.axis_size("tm")
    each = plant_dual.shape[1]
    total_skus = width * skus
    owner = lax.axis_index("sku") * each
    cost = unit_cost.reshape(1, width)
    holding = holding_cost.reshape(1, width)
    load = load_coef.reshape(1, width)
    plant_row = plants.reshape(1, width)

    y_next = shifted(balance_dual, "tm", -1)
    padded = jnp.pad(plant_dual, ((0, 0), (0, P_SIZE - each)))
    gathered = spread(jnp.broadcast_to(padded[None], (skus, ROWS, P_SIZE)), "sku")
    v_next = shifted(stock_v, "tm", -1)
    d_next = shifted(demand, "tm", -1)
    prev_rows = shifted(jnp.concatenate([stock_v[7:8], balance_dual[7:8]], 0), "tm", 1)
    far_rows = shifted(jnp.concatenate([balance_dual[0:2], stock_v[0:1], demand[0:1]], 0), "tm", -2)

    x1, bar1, loads1, prices0 = call(
        first_kernel,
        (shape(ROWS, width), shape(ROWS, width), shape(skus, ROWS, P_SIZE), shape(ROWS, P_SIZE)),
        (step_codes, lags, gathered, primal_x, balance_dual, y_next, cost, load, plant_row),
        smem=2,
        name="first",
    )
    sums1 = spread(loads1, "sku")
    bar_prev = shifted(bar1, "tm", 1)
    bar_row = shifted(bar1[0:1], "tm", -1)
    v2, y1, partial, edge, dual_x, field_x, squares = call(
        middle_kernel,
        (shape(ROWS, width),) * 3
        + (shape(1, width), shape(ROWS, width), shape(ROWS, width), shape(ROWS, BLOCK)),
        (
            step_codes, lags, x1, bar1, bar_prev, bar_row, stock_v, v_next, balance_dual, y_next,
            demand, d_next, prev_rows, far_rows, holding,
        ),
        smem=2,
        name="middle",
    )
    edge_prev = shifted(edge, "tm", 1)
    x2, bar2, loads2, prices1, above1 = call(
        second_kernel,
        (
            shape(ROWS, width), shape(ROWS, width), shape(skus, 3 * ROWS, P_SIZE),
            shape(ROWS, P_SIZE), shape(ROWS, P_SIZE),
        ),
        (
            step_codes, lags, sums1, prices0, capacity, x1, dual_x, field_x, squares, cost, load,
            plant_row,
        ),
        smem=2,
        name="second",
    )
    sums2 = spread(loads2, "sku")
    bar2_prev = shifted(bar2, "tm", 1)

    def third(*refs):
        third_kernel(*refs, total_skus=total_skus)

    prices2, packed = call(
        third,
        (shape(ROWS, P_SIZE), shape(times, ROWS, P_SIZE)),
        (step_codes, sums2, prices1, capacity, above1),
        smem=1,
        name="third",
    )
    portion = lax.dynamic_slice_in_dim(prices2, owner, each, 1)
    gathered2 = spread(packed, "tm")

    def last(*refs):
        last_kernel(*refs, cells=ROWS * times * total_skus, rows_all=ROWS * times * P_SIZE)

    residuals = call(last, shape(2, 2), (gathered2,), out_specs=SMEM, name="last")
    next_y = call(
        dual_kernel,
        shape(ROWS, width),
        (step_codes, lags, y1, partial, edge_prev, bar2, bar2_prev),
        smem=2,
        name="dual",
    )
    return x2, v2, next_y, portion, residuals


def solution(mesh):
    return jax.shard_map(
        body,
        mesh=mesh,
        in_specs=(
            P("tm", "sku"),
            P("tm", "sku"),
            P("tm", "sku"),
            P("tm", "sku"),
            P("tm", "sku"),
            P("sku"),
            P("sku"),
            P("sku"),
            P("tm", None),
            P("sku"),
            P("sku"),
            P(),
        ),
        out_specs=(P("tm", "sku"), P("tm", "sku"), P("tm", "sku"), P("tm", "sku"), P()),
        check_vma=False,
    )
```

```python
import jax
import jax.numpy as jnp
from jax import lax
from jax.experimental import pallas as pl
from jax.experimental.pallas import tpu as pltpu
from jax.sharding import PartitionSpec as P

P_SIZE = 128
LAGMAX = 8
BLOCK = 128
ROWS = 8
F32 = jnp.float32
VMEM = pl.BlockSpec(memory_space=pltpu.VMEM)
SMEM = pl.BlockSpec(memory_space=pltpu.SMEM)


def shifted(value, axis, steps):
    count = lax.axis_size(axis)
    return lax.ppermute(value, axis, [(i, (i + steps) % count) for i in range(count)])


def spread(value, axis):
    return lax.all_to_all(value, axis, 0, 0, tiled=True)


def shape(*dims):
    return jax.ShapeDtypeStruct(dims, F32)


def call(kernel, out_shape, operands, smem=0, out_specs=None, name=None, grant=16):
    size = sum(o.size * 4 for o in operands)
    outs = out_shape if isinstance(out_shape, tuple) else (out_shape,)
    size += sum(o.size * 4 for o in outs)
    return pl.pallas_call(
        kernel,
        out_shape=out_shape,
        in_specs=[SMEM] * smem + [VMEM] * (len(operands) - smem),
        out_specs=out_specs if out_specs is not None else jax.tree.map(lambda _: VMEM, out_shape),
        cost_estimate=pl.CostEstimate(flops=20 * size, bytes_accessed=size, transcendentals=0),
        name=name,
        compiler_params=pltpu.CompilerParams(vmem_limit_bytes=grant * 2**20),
    )(*operands)


def step_size(codes, index):
    return 0.05 * (codes[index].astype(F32) + 2.0)


def row_ids():
    return lax.broadcasted_iota(jnp.int32, (ROWS, BLOCK), 0)


def wide(row):
    return jnp.broadcast_to(row, (ROWS, BLOCK))


def ahead(own, after, lag, rows):
    return pltpu.roll(jnp.where(rows >= lag, own, after), ROWS - lag, 0)


def past(own, before, lag, rows):
    return pltpu.roll(jnp.where(rows < ROWS - lag, own, before), lag & (ROWS - 1), 0)


def row_after(own, last, rows):
    return jnp.where(rows == ROWS - 1, last, pltpu.roll(own, ROWS - 1, 0))


def row_before(own, first, rows):
    return jnp.where(rows == 0, first, pltpu.roll(own, 1, 0))


def stock_step(stock, cost, dual, dual_after, primal):
    return jnp.maximum(stock - primal * (cost - dual + dual_after), 0.0)


def price_of(prices, plant_row):
    return jnp.take_along_axis(prices, wide(plant_row), axis=1, mode="promise_in_bounds")


def load_terms(values, plant_row, plant_ids):
    high = values.astype(jnp.bfloat16).astype(F32)
    rest = values - high
    middle = rest.astype(jnp.bfloat16).astype(F32)
    pieces = jnp.concatenate([high, middle, rest - middle], 0).astype(jnp.bfloat16)
    table = jnp.where(plant_ids == plant_row, 1.0, 0.0).astype(jnp.bfloat16)
    return lax.dot_general(table, pieces, (((1,), (1,)), ((), ())), preferred_element_type=F32)


def folded(total):
    total = total.T
    return total[0:8] + total[8:16] + total[16:24]


def blocks(width):
    return [(i, pl.ds(i * BLOCK, BLOCK)) for i in range(width // BLOCK)]


def extra_slot(index, width, slot):
    each = width // ROWS // BLOCK
    start = width + slot * (width // ROWS) + (index % each) * BLOCK
    return slice(index // each, index // each + 1), slice(start, start + BLOCK)


def start_kernel(w, y, v, d, payload, sent, stock):
    width = y.shape[1]
    each = w.shape[1]
    payload[:, 0:ROWS, 0:each] = jnp.broadcast_to(w[...][None], (payload.shape[0], ROWS, each))
    sent[:, 0:width] = y[...]
    stock[:, 0:width] = v[...]
    for i, at in blocks(width):
        sent[extra_slot(i, width, 0)] = v[0:1, at]
        sent[extra_slot(i, width, 1)] = d[0:1, at]
        stock[extra_slot(i, width, 0)] = d[0:1, at]
        stock[extra_slot(i, width, 1)] = d[1:2, at]


def first_kernel(
    codes, lags, gathered, x, y, y_next, v, d, cost, holding, load, plants, cap,
    x1, up, down, loads, prices, limits,
):
    primal = step_size(codes, 0)
    rows = row_ids()
    plant_ids = lax.broadcasted_iota(jnp.int32, (P_SIZE, BLOCK), 0)
    width = x.shape[1]
    each = P_SIZE // gathered.shape[0]
    for j in range(gathered.shape[0]):
        prices[:, j * each : (j + 1) * each] = gathered[j, 0:ROWS, 0:each]
    w = prices[...]
    limits[...] = cap[...]
    total = jnp.zeros((P_SIZE, 3 * ROWS), F32)
    for i, at in blocks(width):
        lag = lags[i]
        yb = y_next[:, at]
        dual = ahead(y[:, at], yb, lag, rows)
        old = x[:, at]
        charged = price_of(w, plants[:, at]) * load[:, at]
        new = jnp.maximum(old - primal * (cost[:, at] + dual + charged), 0.0)
        over = 2.0 * new - old
        x1[:, at] = new
        total += load_terms(over * load[:, at], plants[:, at], plant_ids)
        v7, v8 = v[7:8, at], y_next[extra_slot(i, width, 0)]
        d8 = y_next[extra_slot(i, width, 1)]
        bar7 = 2.0 * stock_step(v7, holding[:, at], y[7:8, at], yb[0:1], primal) - v7
        bar8 = 2.0 * stock_step(v8, holding[:, at], yb[0:1], yb[1:2], primal) - v8
        up[:, at] = over
        up[extra_slot(i, width, 0)] = bar7
        first_row = over[0:1] + jnp.where(lag == LAGMAX, -d8 - bar8 + bar7, 0.0)
        down[:, at] = jnp.where(rows == 0, first_row, jnp.where(rows == 1, yb[0:1], d[:, at]))
    loads[...] = jnp.broadcast_to(folded(total)[None], loads.shape)


def middle_kernel(
    codes, lags, bar, bar_prev, after, y, y_next, v, v_next, d, holding,
    v2, dual_x, field_x, squares,
):
    primal = step_size(codes, 0)
    dual_step = step_size(codes, 1)
    rows = row_ids()
    width = v.shape[1]
    square = jnp.zeros((ROWS, BLOCK), F32)
    for i, at in blocks(width):
        lag = lags[i]
        cost = holding[:, at]
        ya, yb = y[:, at], y_next[:, at]
        va, vb = v[:, at], v_next[:, at]
        da, mixed = d[:, at], after[:, at]
        d8, d9 = v_next[extra_slot(i, width, 0)], v_next[extra_slot(i, width, 1)]
        bar8, y16 = mixed[0:1], mixed[1:2]
        db = jnp.where(rows == 0, d8, jnp.where(rows == 1, d9, mixed))
        bar_before = bar_prev[extra_slot(i, width, 0)]
        over = bar[:, at]
        va1 = stock_step(va, cost, ya, row_after(ya, yb[0:1], rows), primal)
        vb1 = stock_step(vb, cost, yb, row_after(yb, y16, rows), primal)
        va_bar = 2.0 * va1 - va
        vb_bar = 2.0 * vb1 - vb
        ha = -da - va_bar + row_before(va_bar, bar_before, rows)
        hb = -db - vb_bar + row_before(vb_bar, va_bar[7:8], rows)
        misfit = ahead(ha, hb, lag, rows) + over
        square += misfit * misfit
        yx = ahead(ya, yb, lag, rows) + dual_step * misfit
        dual_x[:, at] = yx
        ya1 = ya + dual_step * (ha + past(over, bar_prev[:, at], lag, rows))
        y8 = yb[0:1] + dual_step * (hb[0:1] + pltpu.roll(over, lag & (ROWS - 1), 0)[0:1])
        va2 = stock_step(va1, cost, ya1, row_after(ya1, y8, rows), primal)
        v2[:, at] = va2
        start_bar = pltpu.roll(2.0 * va2 - va1, ROWS - lag + 1, 0)[0:1]
        whole = lag == LAGMAX
        y_end = jnp.where(whole, y16, pltpu.roll(yb, ROWS - lag, 0)[0:1])
        h_end = jnp.where(whole, 0.0, pltpu.roll(hb, ROWS - lag, 0)[0:1])
        yx_end = y_end + dual_step * (h_end + bar8)
        vx1 = ahead(va1, vb1, lag, rows)
        vx2 = stock_step(vx1, cost, yx, row_after(yx, yx_end, rows), primal)
        vx_bar = 2.0 * vx2 - vx1
        dx = ahead(da, db, lag, rows)
        field_x[:, at] = -dx - vx_bar + row_before(vx_bar, start_bar, rows)
    squares[...] = jnp.sum(square, axis=0, keepdims=True)


def second_kernel(
    codes, sums, prices, cap, x, dual, field, squares, cost, load, plants,
    x2, dual_x, loads, prices_new, excess_row,
):
    primal = step_size(codes, 0)
    dual_step = step_size(codes, 1)
    plant_step = dual_step * (P_SIZE / (x.shape[1] * sums.shape[0]))
    plant_ids = lax.broadcasted_iota(jnp.int32, (P_SIZE, BLOCK), 0)
    excess = jnp.sum(sums[...], axis=0) - cap[...]
    w = jnp.maximum(prices[...] + plant_step * excess, 0.0)
    prices_new[...] = w
    above = jnp.maximum(excess, 0.0)
    excess_row[...] = jnp.sum(above * above, axis=0, keepdims=True)
    total = jnp.zeros((P_SIZE, 3 * ROWS), F32)
    square = jnp.zeros((ROWS, BLOCK), F32)
    for i, at in blocks(x.shape[1]):
        old = x[:, at]
        charged = price_of(w, plants[:, at]) * load[:, at]
        new = jnp.maximum(old - primal * (cost[:, at] + dual[:, at] + charged), 0.0)
        over = 2.0 * new - old
        x2[:, at] = new
        misfit = field[:, at] + over
        dual_x[:, at] = dual[:, at] + dual_step * misfit
        square += misfit * misfit
        total += load_terms(over * load[:, at], plants[:, at], plant_ids)
    count = loads.shape[0]
    lines = jnp.concatenate([squares[...], jnp.sum(square, axis=0, keepdims=True)] * 4, 0)
    loads[:, 0:8, :] = jnp.broadcast_to(folded(total)[None], (count, ROWS, P_SIZE))
    loads[:, 8:16, :] = jnp.broadcast_to(lines[None], (count, ROWS, P_SIZE))


def third_kernel(codes, sums, prices, cap, excess_row, price_out, out, *, total_skus):
    plant_step = step_size(codes, 1) * (P_SIZE / total_skus)
    totals = jnp.sum(sums[...], axis=0)
    excess = totals[0:8] - cap[...]
    price_out[...] = jnp.maximum(prices[...] + plant_step * excess, 0.0)
    above = jnp.maximum(excess, 0.0)
    above_row = jnp.sum(above * above, axis=0, keepdims=True)
    packed = jnp.concatenate([totals[8:9], excess_row[...], totals[9:10], above_row] * 2, 0)
    out[...] = jnp.broadcast_to(packed[None], out.shape)


def unshift_kernel(lags, dual, dual_prev, y):
    rows = row_ids()
    for i, at in blocks(y.shape[1]):
        y[:, at] = past(dual[:, at], dual_prev[:, at], lags[i], rows)


def body(
    primal_x,
    stock_v,
    balance_dual,
    plant_dual,
    demand,
    unit_cost,
    holding_cost,
    load_coef,
    capacity,
    lags,
    plants,
    step_codes,
):
    width = primal_x.shape[1]
    skus = lax.axis_size("sku")
    times = lax.axis_size("tm")
    each = plant_dual.shape[1]
    total_skus = width * skus
    owner = lax.axis_index("sku") * each
    cost = unit_cost.reshape(1, width)
    holding = holding_cost.reshape(1, width)
    load = load_coef.reshape(1, width)
    plant_row = plants.reshape(1, width)

    longer = width + 2 * (width // ROWS)
    payload, y_sent, v_sent = call(
        start_kernel,
        (shape(skus, 2 * ROWS, P_SIZE), shape(ROWS, longer), shape(ROWS, longer)),
        (plant_dual, balance_dual, stock_v, demand),
        name="start",
        grant=60,
    )
    gathered = spread(payload, "sku")
    y_next = shifted(y_sent, "tm", -1)
    v_next = shifted(v_sent, "tm", -1)

    x1, up, down, loads1, prices0, limits = call(
        first_kernel,
        (
            shape(ROWS, width), shape(ROWS, width + width // ROWS), shape(ROWS, width),
            shape(skus, ROWS, P_SIZE), shape(ROWS, P_SIZE), shape(ROWS, P_SIZE),
        ),
        (
            step_codes, lags, gathered, primal_x, balance_dual, y_next, stock_v, demand, cost,
            holding, load, plant_row, capacity,
        ),
        smem=2,
        name="first",
        grant=60,
    )
    bar_prev = shifted(up, "tm", 1)
    after = shifted(down, "tm", -1)
    sums1 = spread(loads1, "sku")
    v2, dual_x, field_x, squares = call(
        middle_kernel,
        (shape(ROWS, width),) * 3 + (shape(1, BLOCK),),
        (
            step_codes, lags, up, bar_prev, after, balance_dual, y_next, stock_v, v_next, demand,
            holding,
        ),
        smem=2,
        name="middle",
    )
    x2, dual_x2, loads2, prices1, above1 = call(
        second_kernel,
        (
            shape(ROWS, width), shape(ROWS, width), shape(skus, 2 * ROWS, P_SIZE),
            shape(ROWS, P_SIZE), shape(1, P_SIZE),
        ),
        (
            step_codes, sums1, prices0, limits, x1, dual_x, field_x, squares, cost, load,
            plant_row,
        ),
        smem=1,
        name="second",
    )
    sums2 = spread(loads2, "sku")
    dual_prev = shifted(dual_x2, "tm", 1)

    def third(*refs):
        third_kernel(*refs, total_skus=total_skus)

    prices2, packed = call(
        third,
        (shape(ROWS, P_SIZE), shape(times, ROWS, P_SIZE)),
        (step_codes, sums2, prices1, limits, above1),
        smem=1,
        name="third",
    )
    portion = lax.dynamic_slice_in_dim(prices2, owner, each, 1)
    totals = jnp.sum(spread(packed, "tm")[:, 0:4], axis=(0, 2))
    scale = P_SIZE / total_skus
    cells, cap_rows = ROWS * times * total_skus, ROWS * times * P_SIZE
    factors = jnp.array([1.0 / cells, scale * scale / cap_rows] * 2, F32)
    residuals = (totals * factors).reshape(2, 2)
    next_y = call(
        unshift_kernel, shape(ROWS, width), (lags, dual_x2, dual_prev), smem=1, name="unshift"
    )
    return x2, v2, next_y, portion, residuals


def solution(mesh):
    return jax.shard_map(
        body,
        mesh=mesh,
        in_specs=(
            P("tm", "sku"),
            P("tm", "sku"),
            P("tm", "sku"),
            P("tm", "sku"),
            P("tm", "sku"),
            P("sku"),
            P("sku"),
            P("sku"),
            P("tm", None),
            P("sku"),
            P("sku"),
            P(),
        ),
        out_specs=(P("tm", "sku"), P("tm", "sku"), P("tm", "sku"), P("tm", "sku"), P()),
        check_vma=False,
    )
```

```python
import math

import jax
import jax.numpy as jnp
from jax import lax
from jax.experimental import pallas as pl
from jax.experimental.pallas import tpu as pltpu
from jax.sharding import PartitionSpec as P

P_SIZE = 128
LAGMAX = 8
BLOCK = 128
ROWS = 8
F32 = jnp.float32
VMEM = pl.BlockSpec(memory_space=pltpu.VMEM)
SMEM = pl.BlockSpec(memory_space=pltpu.SMEM)


def shifted(value, axis, steps):
    count = lax.axis_size(axis)
    return lax.ppermute(value, axis, [(i, (i + steps) % count) for i in range(count)])


def swapped(value, axis, first):
    count = lax.axis_size(axis)
    pairs = [(i, (i + 1 if (i - first) % 2 == 0 else i - 1) % count) for i in range(count)]
    return lax.ppermute(value, axis, pairs)


def spread(value, axis):
    return lax.all_to_all(value, axis, 0, 0, tiled=True)


def shape(*dims):
    return jax.ShapeDtypeStruct(dims, F32)


def near(*dims, dtype=F32):
    return pltpu.VMEM(dims, dtype)


def call(kernel, out_shape, operands, smem=0, name=None, grant=16):
    outs = out_shape if isinstance(out_shape, tuple) else (out_shape,)
    size = sum(4 * math.prod(o.shape) for o in (*operands, *outs))
    return pl.pallas_call(
        kernel,
        out_shape=out_shape,
        in_specs=[SMEM] * smem + [VMEM] * (len(operands) - smem),
        out_specs=(VMEM,) * len(out_shape) if isinstance(out_shape, tuple) else VMEM,
        cost_estimate=pl.CostEstimate(flops=20 * size, bytes_accessed=size, transcendentals=0),
        name=name,
        compiler_params=pltpu.CompilerParams(vmem_limit_bytes=grant * 2**20),
    )(*operands)


def step_size(codes, index):
    return 0.05 * (codes[index].astype(F32) + 2.0)


def row_ids():
    return lax.broadcasted_iota(jnp.int32, (ROWS, BLOCK), 0)


def wide(row):
    return jnp.broadcast_to(row, (ROWS, BLOCK))


def ahead(own, after, lag, rows):
    return pltpu.roll(jnp.where(rows >= lag, own, after), ROWS - lag, 0)


def past(own, before, lag, rows):
    return pltpu.roll(jnp.where(rows < ROWS - lag, own, before), lag & (ROWS - 1), 0)


def row_after(own, last, rows):
    return jnp.where(rows == ROWS - 1, last, pltpu.roll(own, ROWS - 1, 0))


def row_before(own, first, rows):
    return jnp.where(rows == 0, first, pltpu.roll(own, 1, 0))


def stock_step(stock, cost, dual, dual_after, primal):
    return jnp.maximum(stock - primal * (cost - dual + dual_after), 0.0)


def price_of(prices, plant_row):
    return jnp.take_along_axis(prices, wide(plant_row), axis=1, mode="promise_in_bounds")


def load_terms(values, plant_row, plant_ids):
    high = values.astype(jnp.bfloat16).astype(F32)
    rest = values - high
    middle = rest.astype(jnp.bfloat16).astype(F32)
    pieces = jnp.concatenate([high, middle, rest - middle], 0).astype(jnp.bfloat16)
    table = jnp.where(plant_ids == plant_row, 1.0, 0.0).astype(jnp.bfloat16)
    return lax.dot_general(table, pieces, (((1,), (1,)), ((), ())), preferred_element_type=F32)


def folded(total):
    total = total.T
    return total[0:8] + total[8:16] + total[16:24]


def blocks(width):
    return [(i, pl.ds(i * BLOCK, BLOCK)) for i in range(width // BLOCK)]


def extra_slot(index, width, slot):
    each = width // ROWS // BLOCK
    start = width + slot * (width // ROWS) + (index % each) * BLOCK
    return slice(index // each, index // each + 1), slice(start, start + BLOCK)


def start_kernel(w, y, v, d, payload, sent):
    width = y.shape[1]
    each = w.shape[1]
    payload[:, 0:ROWS, 0:each] = jnp.broadcast_to(w[...][None], (payload.shape[0], ROWS, each))
    sent[:, 0:width] = y[...]
    for i, at in blocks(width):
        sent[extra_slot(i, width, 0)] = v[0:1, at]
        sent[extra_slot(i, width, 1)] = d[0:1, at]


def stage(scalars, v, d, others):
    operands = (*scalars, v, d, *others)
    count, at_v = len(operands), len(scalars)

    def kernel(*refs):
        outs, sent, sems = refs[count : 2 * count], refs[2 * count], refs[2 * count + 1]
        copies = [pltpu.make_async_copy(refs[i], outs[i], sems.at[i]) for i in range(count)]
        for copy in copies:
            copy.start()
        for copy in copies:
            copy.wait()
        v, d = outs[at_v], outs[at_v + 1]
        width = v.shape[1]
        sent[:, 0:width] = v[...]
        for i, at in blocks(width):
            sent[extra_slot(i, width, 0)] = d[0:1, at]
            sent[extra_slot(i, width, 1)] = d[1:2, at]

    width = v.shape[1]
    return pl.pallas_call(
        kernel,
        out_shape=tuple(pltpu.SMEM(o.shape, o.dtype) for o in scalars)
        + tuple(near(*o.shape, dtype=o.dtype) for o in operands[at_v:])
        + (near(ROWS, width + 2 * (width // ROWS)),),
        in_specs=[pl.BlockSpec(memory_space=pltpu.HBM)] * count,
        out_specs=(SMEM,) * at_v + (VMEM,) * (count - at_v + 1),
        scratch_shapes=[pltpu.SemaphoreType.DMA((count,))],
        name="stage",
        compiler_params=pltpu.CompilerParams(vmem_limit_bytes=16 * 2**20),
    )(*(pltpu.with_memory_space_constraint(o, pltpu.HBM) for o in operands))


def first_kernel(
    codes, lags, gathered, x, y, y_next, v, d, cost, holding, load, plants,
    x1, inner, outer, loads, prices,
):
    primal = step_size(codes, 0)
    rows = row_ids()
    plant_ids = lax.broadcasted_iota(jnp.int32, (P_SIZE, BLOCK), 0)
    odd = codes[2] == 1
    width = x.shape[1]
    each = P_SIZE // gathered.shape[0]
    for j in range(gathered.shape[0]):
        prices[:, j * each : (j + 1) * each] = gathered[j, 0:ROWS, 0:each]
    w = prices[...]
    total = jnp.zeros((P_SIZE, 3 * ROWS), F32)
    for i, at in blocks(width):
        lag = lags[i]
        yb = y_next[:, at]
        dual = ahead(y[:, at], yb, lag, rows)
        old = x[:, at]
        charged = price_of(w, plants[:, at]) * load[:, at]
        new = jnp.maximum(old - primal * (cost[:, at] + dual + charged), 0.0)
        over = 2.0 * new - old
        x1[:, at] = new
        total += load_terms(over * load[:, at], plants[:, at], plant_ids)
        v7, v8 = v[7:8, at], y_next[extra_slot(i, width, 0)]
        d8 = y_next[extra_slot(i, width, 1)]
        bar7 = 2.0 * stock_step(v7, holding[:, at], y[7:8, at], yb[0:1], primal) - v7
        bar8 = 2.0 * stock_step(v8, holding[:, at], yb[0:1], yb[1:2], primal) - v8
        first_row = over[0:1] + jnp.where(lag == LAGMAX, -d8 - bar8 + bar7, 0.0)
        down = jnp.where(rows == 0, first_row, jnp.where(rows == 1, yb[0:1], d[:, at]))
        inner[:, at] = jnp.where(odd, down, over)
        outer[:, at] = jnp.where(odd, over, down)
        inner[extra_slot(i, width, 0)] = bar7
        outer[extra_slot(i, width, 0)] = bar7
    loads[...] = jnp.broadcast_to(folded(total)[None], loads.shape)


def middle_kernel(
    codes, lags, x, x1, inner, outer, y, y_next, v, v_next, d, holding,
    v2, dual_x, field_x,
):
    primal = step_size(codes, 0)
    dual_step = step_size(codes, 1)
    rows = row_ids()
    odd = codes[2] == 1
    width = v.shape[1]
    square = jnp.zeros((ROWS, BLOCK), F32)
    for i, at in blocks(width):
        lag = lags[i]
        cost = holding[:, at]
        ya, yb = y[:, at], y_next[:, at]
        va, vb = v[:, at], v_next[:, at]
        pair = inner[:, at], outer[:, at]
        bar_prev, mixed = jnp.where(odd, *pair), jnp.where(odd, *pair[::-1])
        da = d[:, at]
        d8, d9 = v_next[extra_slot(i, width, 0)], v_next[extra_slot(i, width, 1)]
        bar8, y16 = mixed[0:1], mixed[1:2]
        db = jnp.where(rows == 0, d8, jnp.where(rows == 1, d9, mixed))
        slot = extra_slot(i, width, 0)
        bar_before = jnp.where(odd, inner[slot], outer[slot])
        over = 2.0 * x1[:, at] - x[:, at]
        va1 = stock_step(va, cost, ya, row_after(ya, yb[0:1], rows), primal)
        vb1 = stock_step(vb, cost, yb, row_after(yb, y16, rows), primal)
        va_bar = 2.0 * va1 - va
        vb_bar = 2.0 * vb1 - vb
        ha = -da - va_bar + row_before(va_bar, bar_before, rows)
        hb = -db - vb_bar + row_before(vb_bar, va_bar[7:8], rows)
        misfit = ahead(ha, hb, lag, rows) + over
        square += misfit * misfit
        yx = ahead(ya, yb, lag, rows) + dual_step * misfit
        dual_x[:, at] = yx
        ya1 = ya + dual_step * (ha + past(over, bar_prev, lag, rows))
        y8 = yb[0:1] + dual_step * (hb[0:1] + pltpu.roll(over, lag & (ROWS - 1), 0)[0:1])
        va2 = stock_step(va1, cost, ya1, row_after(ya1, y8, rows), primal)
        v2[:, at] = va2
        start_bar = pltpu.roll(2.0 * va2 - va1, ROWS - lag + 1, 0)[0:1]
        whole = lag == LAGMAX
        y_end = jnp.where(whole, y16, pltpu.roll(yb, ROWS - lag, 0)[0:1])
        h_end = jnp.where(whole, 0.0, pltpu.roll(hb, ROWS - lag, 0)[0:1])
        yx_end = y_end + dual_step * (h_end + bar8)
        vx1 = ahead(va1, vb1, lag, rows)
        vx2 = stock_step(vx1, cost, yx, row_after(yx, yx_end, rows), primal)
        vx_bar = 2.0 * vx2 - vx1
        dx = ahead(da, db, lag, rows)
        field_x[:, at] = -dx - vx_bar + row_before(vx_bar, start_bar, rows)
    field_x[:, width : width + BLOCK] = square


def second_kernel(
    codes, sums, prices, cap, x, dual, field, cost, load, plants,
    x2, dual_x, loads, prices_new, excess_row,
):
    primal = step_size(codes, 0)
    dual_step = step_size(codes, 1)
    plant_step = dual_step * (P_SIZE / (x.shape[1] * sums.shape[0]))
    plant_ids = lax.broadcasted_iota(jnp.int32, (P_SIZE, BLOCK), 0)
    excess = jnp.sum(sums[...], axis=0) - cap[...]
    w = jnp.maximum(prices[...] + plant_step * excess, 0.0)
    prices_new[...] = w
    above = jnp.maximum(excess, 0.0)
    excess_row[...] = jnp.sum(above * above, axis=0, keepdims=True)
    total = jnp.zeros((P_SIZE, 3 * ROWS), F32)
    square = jnp.zeros((ROWS, BLOCK), F32)
    for i, at in blocks(x.shape[1]):
        old = x[:, at]
        charged = price_of(w, plants[:, at]) * load[:, at]
        new = jnp.maximum(old - primal * (cost[:, at] + dual[:, at] + charged), 0.0)
        over = 2.0 * new - old
        x2[:, at] = new
        misfit = field[:, at] + over
        dual_x[:, at] = dual[:, at] + dual_step * misfit
        square += misfit * misfit
        total += load_terms(over * load[:, at], plants[:, at], plant_ids)
    count = loads.shape[0]
    pair = (field[:, x.shape[1] :], square)
    lines = jnp.concatenate([jnp.sum(p, axis=0, keepdims=True) for p in pair] * 4, 0)
    loads[:, 0:8, :] = jnp.broadcast_to(folded(total)[None], (count, ROWS, P_SIZE))
    loads[:, 8:16, :] = jnp.broadcast_to(lines[None], (count, ROWS, P_SIZE))


def third_kernel(codes, sums, prices, cap, excess_row, price_out, out, *, total_skus):
    plant_step = step_size(codes, 1) * (P_SIZE / total_skus)
    totals = jnp.sum(sums[...], axis=0)
    excess = totals[0:8] - cap[...]
    price_out[...] = jnp.maximum(prices[...] + plant_step * excess, 0.0)
    above = jnp.maximum(excess, 0.0)
    above_row = jnp.sum(above * above, axis=0, keepdims=True)
    for k, rows in enumerate(((totals[8:9], excess_row[...]), (totals[9:10], above_row))):
        pair = jnp.concatenate(rows, 0)
        out[:, k] = jnp.broadcast_to(pair[None], (out.shape[0],) + pair.shape)


def unshift_kernel(lags, dual, dual_prev, y):
    rows = row_ids()
    for i, at in blocks(y.shape[1]):
        y[:, at] = past(dual[:, at], dual_prev[:, at], lags[i], rows)


def body(
    primal_x,
    stock_v,
    balance_dual,
    plant_dual,
    demand,
    unit_cost,
    holding_cost,
    load_coef,
    capacity,
    lags,
    plants,
    step_codes,
):
    width = primal_x.shape[1]
    skus = lax.axis_size("sku")
    times = lax.axis_size("tm")
    each = plant_dual.shape[1]
    total_skus = width * skus
    owner = lax.axis_index("sku") * each
    cost = unit_cost.reshape(1, width)
    holding = holding_cost.reshape(1, width)
    load = load_coef.reshape(1, width)
    plant_row = plants.reshape(1, width)

    longer = width + 2 * (width // ROWS)
    payload, y_sent = call(
        start_kernel,
        (shape(skus, 2 * ROWS, P_SIZE), shape(ROWS, longer)),
        (plant_dual, balance_dual, stock_v, demand),
        name="start",
        grant=60,
    )
    y_next = shifted(y_sent, "tm", -1)
    payload, codes, lags, v, d, *held = lax.optimization_barrier(
        (
            payload, step_codes, lags, stock_v, demand, primal_x, balance_dual, cost, holding,
            load, plant_row, capacity,
        )
    )
    parity = lax.axis_index("tm") % 2
    codes = jnp.concatenate([codes, parity.astype(jnp.int32)[None]])
    codes, lags, v, d, x, y, cost, holding, load, plant_row, limits, v_sent = stage(
        (codes, lags), v, d, held
    )
    v_next = shifted(v_sent, "tm", -1)
    gathered = spread(payload, "sku")
    x1, inner, outer, loads1, prices0 = call(
        first_kernel,
        (
            near(ROWS, width), near(ROWS, width + width // ROWS),
            near(ROWS, width + width // ROWS), shape(skus, ROWS, P_SIZE), near(ROWS, P_SIZE),
        ),
        (codes, lags, gathered, x, y, y_next, v, d, cost, holding, load, plant_row),
        smem=2,
        name="first",
    )
    inner = swapped(inner, "tm", 0)
    outer = swapped(outer, "tm", 1)
    sums1 = spread(loads1, "sku")
    v2, dual_x, field_x = call(
        middle_kernel,
        (near(ROWS, width), near(ROWS, width), near(ROWS, width + BLOCK)),
        (codes, lags, x, x1, inner, outer, y, y_next, v, v_next, d, holding),
        smem=2,
        name="middle",
    )
    x2, dual_x2, loads2, prices1, above1 = call(
        second_kernel,
        (
            near(ROWS, width), near(ROWS, width), shape(skus, 2 * ROWS, P_SIZE),
            near(ROWS, P_SIZE), near(1, P_SIZE),
        ),
        (
            codes, sums1, prices0, limits, x1, dual_x, field_x, cost, load,
            plant_row,
        ),
        smem=1,
        name="second",
    )
    sums2 = spread(loads2, "sku")
    dual_prev = shifted(dual_x2, "tm", 1)

    def third(*refs):
        third_kernel(*refs, total_skus=total_skus)

    prices2, packed = call(
        third,
        (near(ROWS, P_SIZE), shape(times, 2, 2, P_SIZE)),
        (codes, sums2, prices1, limits, above1),
        smem=1,
        name="third",
    )
    portion = lax.dynamic_slice_in_dim(prices2, owner, each, 1)
    totals = jnp.sum(spread(packed, "tm"), axis=(0, 3))
    scale = P_SIZE / total_skus
    cells, cap_rows = ROWS * times * total_skus, ROWS * times * P_SIZE
    column = lax.broadcasted_iota(jnp.int32, totals.shape, 1)
    residuals = totals * jnp.where(column == 0, 1.0 / cells, scale * scale / cap_rows)
    next_y = call(
        unshift_kernel, shape(ROWS, width), (lags, dual_x2, dual_prev), smem=1, name="unshift"
    )
    return x2, v2, next_y, portion, residuals


def solution(mesh):
    return jax.shard_map(
        body,
        mesh=mesh,
        in_specs=(
            P("tm", "sku"),
            P("tm", "sku"),
            P("tm", "sku"),
            P("tm", "sku"),
            P("tm", "sku"),
            P("sku"),
            P("sku"),
            P("sku"),
            P("tm", None),
            P("sku"),
            P("sku"),
            P(),
        ),
        out_specs=(P("tm", "sku"), P("tm", "sku"), P("tm", "sku"), P("tm", "sku"), P()),
        check_vma=False,
    )
```

```python
import math

import jax
import jax.numpy as jnp
from jax import lax
from jax.experimental import pallas as pl
from jax.experimental.pallas import tpu as pltpu
from jax.sharding import PartitionSpec as P

P_SIZE = 128
LAGMAX = 8
BLOCK = 128
ROWS = 8
F32 = jnp.float32
VMEM = pl.BlockSpec(memory_space=pltpu.VMEM)
SMEM = pl.BlockSpec(memory_space=pltpu.SMEM)


def shifted(value, axis, steps):
    count = lax.axis_size(axis)
    return lax.ppermute(value, axis, [(i, (i + steps) % count) for i in range(count)])


def swapped(value, axis, first):
    count = lax.axis_size(axis)
    pairs = [(i, (i + 1 if (i - first) % 2 == 0 else i - 1) % count) for i in range(count)]
    return lax.ppermute(value, axis, pairs)


def spread(value, axis):
    return lax.all_to_all(value, axis, 0, 0, tiled=True)


def spread_rows(value):
    times, skus = lax.axis_size("tm"), lax.axis_size("sku")
    half = skus // 2
    groups = [
        [t * skus + (side ^ (t // 2 % 4 < 2)) * half + rest for t in range(times)]
        for side in range(2)
        for rest in range(half)
    ]
    return lax.all_to_all(value, ("tm", "sku"), 0, 0, axis_index_groups=groups, tiled=True)


def shape(*dims):
    return jax.ShapeDtypeStruct(dims, F32)


def near(*dims, dtype=F32):
    return pltpu.VMEM(dims, dtype)


def call(kernel, out_shape, operands, smem=0, name=None, grant=16):
    outs = out_shape if isinstance(out_shape, tuple) else (out_shape,)
    size = sum(4 * math.prod(o.shape) for o in (*operands, *outs))
    return pl.pallas_call(
        kernel,
        out_shape=out_shape,
        in_specs=[SMEM] * smem + [VMEM] * (len(operands) - smem),
        out_specs=(VMEM,) * len(out_shape) if isinstance(out_shape, tuple) else VMEM,
        cost_estimate=pl.CostEstimate(flops=20 * size, bytes_accessed=size, transcendentals=0),
        name=name,
        compiler_params=pltpu.CompilerParams(vmem_limit_bytes=grant * 2**20),
    )(*operands)


def step_size(codes, index):
    return 0.05 * (codes[index].astype(F32) + 2.0)


def row_ids():
    return lax.broadcasted_iota(jnp.int32, (ROWS, BLOCK), 0)


def wide(row):
    return jnp.broadcast_to(row, (ROWS, BLOCK))


def ahead(own, after, lag, rows):
    return pltpu.roll(jnp.where(rows >= lag, own, after), ROWS - lag, 0)


def past(own, before, lag, rows):
    return pltpu.roll(jnp.where(rows < ROWS - lag, own, before), lag & (ROWS - 1), 0)


def row_after(own, last, rows):
    return jnp.where(rows == ROWS - 1, last, pltpu.roll(own, ROWS - 1, 0))


def row_before(own, first, rows):
    return jnp.where(rows == 0, first, pltpu.roll(own, 1, 0))


def stock_step(stock, cost, dual, dual_after, primal):
    return jnp.maximum(stock - primal * (cost - dual + dual_after), 0.0)


def price_of(prices, plant_row):
    return jnp.take_along_axis(prices, wide(plant_row), axis=1, mode="promise_in_bounds")


def load_terms(values, plant_row, plant_ids):
    high = values.astype(jnp.bfloat16).astype(F32)
    rest = values - high
    middle = rest.astype(jnp.bfloat16).astype(F32)
    pieces = jnp.concatenate([high, middle, rest - middle], 0).astype(jnp.bfloat16)
    table = jnp.where(plant_ids == plant_row, 1.0, 0.0).astype(jnp.bfloat16)
    return lax.dot_general(table, pieces, (((1,), (1,)), ((), ())), preferred_element_type=F32)


def folded(total):
    total = total.T
    return total[0:8] + total[8:16] + total[16:24]


def blocks(width):
    return [(i, pl.ds(i * BLOCK, BLOCK)) for i in range(width // BLOCK)]


def extra_slot(index, width, slot):
    each = width // ROWS // BLOCK
    start = width + slot * (width // ROWS) + (index % each) * BLOCK
    return slice(index // each, index // each + 1), slice(start, start + BLOCK)


def start(plant_dual, y, v, d, copies):
    rows, width = y.shape
    each = plant_dual.shape[1]
    parts = 4

    def kernel(w, y, v, d, payload, sent, mine, firsts, filled, sems):
        piece = width // parts
        fetches = [
            pltpu.make_async_copy(w, mine, sems.at[0]),
            pltpu.make_async_copy(v.at[0:1], firsts.at[0], sems.at[1]),
            pltpu.make_async_copy(d.at[0:1], firsts.at[1], sems.at[2]),
        ]
        for k in range(parts):
            at = pl.ds(k * piece, piece)
            fetches.append(pltpu.make_async_copy(y.at[:, at], sent.at[:, at], sems.at[3 + k]))
        for fetch in fetches:
            fetch.start()
        filled[...] = jnp.zeros(filled.shape, F32)
        fetches[0].wait()
        filled[:, 0:rows, 0:each] = jnp.broadcast_to(mine[...][None], (copies, rows, each))
        out = pltpu.make_async_copy(filled, payload, sems.at[3 + parts])
        out.start()
        fetches[1].wait()
        fetches[2].wait()
        for i, at in blocks(width):
            sent[extra_slot(i, width, 0)] = firsts[0, :, at]
            sent[extra_slot(i, width, 1)] = firsts[1, :, at]
        for fetch in fetches[3:]:
            fetch.wait()
        out.wait()

    return pl.pallas_call(
        kernel,
        out_shape=(shape(copies, 2 * rows, P_SIZE), near(rows, width + 2 * (width // rows))),
        in_specs=[pl.BlockSpec(memory_space=pltpu.HBM)] * 4,
        out_specs=(pl.BlockSpec(memory_space=pltpu.HBM), VMEM),
        scratch_shapes=[
            pltpu.VMEM((rows, each), F32),
            pltpu.VMEM((2, 1, width), F32),
            pltpu.VMEM((copies, 2 * rows, P_SIZE), F32),
            pltpu.SemaphoreType.DMA((4 + parts,)),
        ],
        name="start",
        compiler_params=pltpu.CompilerParams(vmem_limit_bytes=16 * 2**20),
    )(*(pltpu.with_memory_space_constraint(o, pltpu.HBM) for o in (plant_dual, y, v, d)))


def stage(scalars, v, d, others):
    operands = (*scalars, v, d, *others)
    count, at_v = len(operands), len(scalars)

    def kernel(*refs):
        outs, sent, sems = refs[count : 2 * count], refs[2 * count], refs[2 * count + 1]
        copies = [pltpu.make_async_copy(refs[i], outs[i], sems.at[i]) for i in range(count)]
        for copy in copies:
            copy.start()
        for copy in copies:
            copy.wait()
        v, d = outs[at_v], outs[at_v + 1]
        width = v.shape[1]
        sent[:, 0:width] = v[...]
        for i, at in blocks(width):
            sent[extra_slot(i, width, 0)] = d[0:1, at]
            sent[extra_slot(i, width, 1)] = d[1:2, at]

    width = v.shape[1]
    return pl.pallas_call(
        kernel,
        out_shape=tuple(pltpu.SMEM(o.shape, o.dtype) for o in scalars)
        + tuple(near(*o.shape, dtype=o.dtype) for o in operands[at_v:])
        + (near(ROWS, width + 2 * (width // ROWS)),),
        in_specs=[pl.BlockSpec(memory_space=pltpu.HBM)] * count,
        out_specs=(SMEM,) * at_v + (VMEM,) * (count - at_v + 1),
        scratch_shapes=[pltpu.SemaphoreType.DMA((count,))],
        name="stage",
        compiler_params=pltpu.CompilerParams(vmem_limit_bytes=16 * 2**20),
    )(*(pltpu.with_memory_space_constraint(o, pltpu.HBM) for o in operands))


def first_kernel(
    codes, lags, gathered, x, y, y_next, v, d, cost, holding, load, plants,
    x1, inner, outer, loads, prices,
):
    primal = step_size(codes, 0)
    rows = row_ids()
    plant_ids = lax.broadcasted_iota(jnp.int32, (P_SIZE, BLOCK), 0)
    odd = codes[2] == 1
    width = x.shape[1]
    each = P_SIZE // gathered.shape[0]
    for j in range(gathered.shape[0]):
        prices[:, j * each : (j + 1) * each] = gathered[j, 0:ROWS, 0:each]
    w = prices[...]
    total = jnp.zeros((P_SIZE, 3 * ROWS), F32)
    for i, at in blocks(width):
        lag = lags[i]
        yb = y_next[:, at]
        dual = ahead(y[:, at], yb, lag, rows)
        old = x[:, at]
        charged = price_of(w, plants[:, at]) * load[:, at]
        new = jnp.maximum(old - primal * (cost[:, at] + dual + charged), 0.0)
        over = 2.0 * new - old
        x1[:, at] = new
        total += load_terms(over * load[:, at], plants[:, at], plant_ids)
        v7, v8 = v[7:8, at], y_next[extra_slot(i, width, 0)]
        d8 = y_next[extra_slot(i, width, 1)]
        bar7 = 2.0 * stock_step(v7, holding[:, at], y[7:8, at], yb[0:1], primal) - v7
        bar8 = 2.0 * stock_step(v8, holding[:, at], yb[0:1], yb[1:2], primal) - v8
        first_row = over[0:1] + jnp.where(lag == LAGMAX, -d8 - bar8 + bar7, 0.0)
        down = jnp.where(rows == 0, first_row, jnp.where(rows == 1, yb[0:1], d[:, at]))
        inner[:, at] = jnp.where(odd, down, over)
        outer[:, at] = jnp.where(odd, over, down)
        inner[extra_slot(i, width, 0)] = bar7
        outer[extra_slot(i, width, 0)] = bar7
    loads[...] = jnp.broadcast_to(folded(total)[None], loads.shape)


def middle_kernel(
    codes, lags, x, x1, inner, outer, y, y_next, v, v_next, d, holding,
    v2, dual_x, field_x,
):
    primal = step_size(codes, 0)
    dual_step = step_size(codes, 1)
    rows = row_ids()
    odd = codes[2] == 1
    width = v.shape[1]
    square = jnp.zeros((ROWS, BLOCK), F32)
    for i, at in blocks(width):
        lag = lags[i]
        cost = holding[:, at]
        ya, yb = y[:, at], y_next[:, at]
        va, vb = v[:, at], v_next[:, at]
        pair = inner[:, at], outer[:, at]
        bar_prev, mixed = jnp.where(odd, *pair), jnp.where(odd, *pair[::-1])
        da = d[:, at]
        d8, d9 = v_next[extra_slot(i, width, 0)], v_next[extra_slot(i, width, 1)]
        bar8, y16 = mixed[0:1], mixed[1:2]
        db = jnp.where(rows == 0, d8, jnp.where(rows == 1, d9, mixed))
        slot = extra_slot(i, width, 0)
        bar_before = jnp.where(odd, inner[slot], outer[slot])
        over = 2.0 * x1[:, at] - x[:, at]
        va1 = stock_step(va, cost, ya, row_after(ya, yb[0:1], rows), primal)
        vb1 = stock_step(vb, cost, yb, row_after(yb, y16, rows), primal)
        va_bar = 2.0 * va1 - va
        vb_bar = 2.0 * vb1 - vb
        ha = -da - va_bar + row_before(va_bar, bar_before, rows)
        hb = -db - vb_bar + row_before(vb_bar, va_bar[7:8], rows)
        misfit = ahead(ha, hb, lag, rows) + over
        square += misfit * misfit
        yx = ahead(ya, yb, lag, rows) + dual_step * misfit
        dual_x[:, at] = yx
        ya1 = ya + dual_step * (ha + past(over, bar_prev, lag, rows))
        y8 = yb[0:1] + dual_step * (hb[0:1] + pltpu.roll(over, lag & (ROWS - 1), 0)[0:1])
        va2 = stock_step(va1, cost, ya1, row_after(ya1, y8, rows), primal)
        v2[:, at] = va2
        start_bar = pltpu.roll(2.0 * va2 - va1, ROWS - lag + 1, 0)[0:1]
        whole = lag == LAGMAX
        y_end = jnp.where(whole, y16, pltpu.roll(yb, ROWS - lag, 0)[0:1])
        h_end = jnp.where(whole, 0.0, pltpu.roll(hb, ROWS - lag, 0)[0:1])
        yx_end = y_end + dual_step * (h_end + bar8)
        vx1 = ahead(va1, vb1, lag, rows)
        vx2 = stock_step(vx1, cost, yx, row_after(yx, yx_end, rows), primal)
        vx_bar = 2.0 * vx2 - vx1
        dx = ahead(da, db, lag, rows)
        field_x[:, at] = -dx - vx_bar + row_before(vx_bar, start_bar, rows)
    field_x[:, width : width + BLOCK] = square


def second_kernel(
    codes, sums, prices, cap, x, dual, field, cost, load, plants,
    x2, dual_x, loads, prices_new, excess_row,
):
    primal = step_size(codes, 0)
    dual_step = step_size(codes, 1)
    plant_step = dual_step * (P_SIZE / (x.shape[1] * sums.shape[0]))
    plant_ids = lax.broadcasted_iota(jnp.int32, (P_SIZE, BLOCK), 0)
    excess = jnp.sum(sums[...], axis=0) - cap[...]
    w = jnp.maximum(prices[...] + plant_step * excess, 0.0)
    prices_new[...] = w
    above = jnp.maximum(excess, 0.0)
    excess_row[...] = jnp.sum(above * above, axis=0, keepdims=True)
    total = jnp.zeros((P_SIZE, 3 * ROWS), F32)
    square = jnp.zeros((ROWS, BLOCK), F32)
    for i, at in blocks(x.shape[1]):
        old = x[:, at]
        charged = price_of(w, plants[:, at]) * load[:, at]
        new = jnp.maximum(old - primal * (cost[:, at] + dual[:, at] + charged), 0.0)
        over = 2.0 * new - old
        x2[:, at] = new
        misfit = field[:, at] + over
        dual_x[:, at] = dual[:, at] + dual_step * misfit
        square += misfit * misfit
        total += load_terms(over * load[:, at], plants[:, at], plant_ids)
    count = loads.shape[0]
    pair = (field[:, x.shape[1] :], square)
    lines = jnp.concatenate([jnp.sum(p, axis=0, keepdims=True) for p in pair] * 4, 0)
    loads[:, 0:8, :] = jnp.broadcast_to(folded(total)[None], (count, ROWS, P_SIZE))
    loads[:, 8:16, :] = jnp.broadcast_to(lines[None], (count, ROWS, P_SIZE))


def third_kernel(codes, sums, prices, cap, excess_row, price_out, out, *, total_skus):
    plant_step = step_size(codes, 1) * (P_SIZE / total_skus)
    totals = jnp.sum(sums[...], axis=0)
    excess = totals[0:8] - cap[...]
    price_out[...] = jnp.maximum(prices[...] + plant_step * excess, 0.0)
    above = jnp.maximum(excess, 0.0)
    above_row = jnp.sum(above * above, axis=0, keepdims=True)
    for k, rows in enumerate(((totals[8:9], excess_row[...]), (totals[9:10], above_row))):
        pair = jnp.concatenate(rows, 0)
        out[:, k] = jnp.broadcast_to(pair[None], (out.shape[0],) + pair.shape)


def unshift_kernel(lags, dual, dual_prev, y):
    rows = row_ids()
    for i, at in blocks(y.shape[1]):
        y[:, at] = past(dual[:, at], dual_prev[:, at], lags[i], rows)


def body(
    primal_x,
    stock_v,
    balance_dual,
    plant_dual,
    demand,
    unit_cost,
    holding_cost,
    load_coef,
    capacity,
    lags,
    plants,
    step_codes,
):
    width = primal_x.shape[1]
    skus = lax.axis_size("sku")
    times = lax.axis_size("tm")
    each = plant_dual.shape[1]
    total_skus = width * skus
    owner = lax.axis_index("sku") * each
    cost = unit_cost.reshape(1, width)
    holding = holding_cost.reshape(1, width)
    load = load_coef.reshape(1, width)
    plant_row = plants.reshape(1, width)

    payload, y_sent = start(plant_dual, balance_dual, stock_v, demand, skus)
    y_next = shifted(y_sent, "tm", -1)
    payload, codes, lags, v, d, *held = lax.optimization_barrier(
        (
            payload, step_codes, lags, stock_v, demand, primal_x, balance_dual, cost, holding,
            load, plant_row, capacity,
        )
    )
    parity = lax.axis_index("tm") % 2
    codes = jnp.concatenate([codes, parity.astype(jnp.int32)[None]])
    codes, lags, v, d, x, y, cost, holding, load, plant_row, limits, v_sent = stage(
        (codes, lags), v, d, held
    )
    v_next = shifted(v_sent, "tm", -1)
    gathered = spread(payload, "sku")
    x1, inner, outer, loads1, prices0 = call(
        first_kernel,
        (
            near(ROWS, width), near(ROWS, width + width // ROWS),
            near(ROWS, width + width // ROWS), shape(skus, ROWS, P_SIZE), near(ROWS, P_SIZE),
        ),
        (codes, lags, gathered, x, y, y_next, v, d, cost, holding, load, plant_row),
        smem=2,
        name="first",
    )
    inner = swapped(inner, "tm", 0)
    outer = swapped(outer, "tm", 1)
    sums1 = spread(loads1, "sku")
    v2, dual_x, field_x = call(
        middle_kernel,
        (near(ROWS, width), near(ROWS, width), near(ROWS, width + BLOCK)),
        (codes, lags, x, x1, inner, outer, y, y_next, v, v_next, d, holding),
        smem=2,
        name="middle",
    )
    x2, dual_x2, loads2, prices1, above1 = call(
        second_kernel,
        (
            near(ROWS, width), near(ROWS, width), shape(skus, 2 * ROWS, P_SIZE),
            near(ROWS, P_SIZE), near(1, P_SIZE),
        ),
        (
            codes, sums1, prices0, limits, x1, dual_x, field_x, cost, load,
            plant_row,
        ),
        smem=1,
        name="second",
    )
    sums2 = spread(loads2, "sku")
    dual_prev = shifted(dual_x2, "tm", 1)

    def third(*refs):
        third_kernel(*refs, total_skus=total_skus)

    prices2, packed = call(
        third,
        (near(ROWS, P_SIZE), shape(times, 2, 2, P_SIZE)),
        (codes, sums2, prices1, limits, above1),
        smem=1,
        name="third",
    )
    portion = lax.dynamic_slice_in_dim(prices2, owner, each, 1)
    totals = jnp.sum(spread_rows(packed), axis=(0, 3))
    scale = P_SIZE / total_skus
    cells, cap_rows = ROWS * times * total_skus, ROWS * times * P_SIZE
    column = lax.broadcasted_iota(jnp.int32, totals.shape, 1)
    residuals = totals * jnp.where(column == 0, 1.0 / cells, scale * scale / cap_rows)
    next_y = call(
        unshift_kernel, shape(ROWS, width), (lags, dual_x2, dual_prev), smem=1, name="unshift"
    )
    return x2, v2, next_y, portion, residuals


def solution(mesh):
    return jax.shard_map(
        body,
        mesh=mesh,
        in_specs=(
            P("tm", "sku"),
            P("tm", "sku"),
            P("tm", "sku"),
            P("tm", "sku"),
            P("tm", "sku"),
            P("sku"),
            P("sku"),
            P("sku"),
            P("tm", None),
            P("sku"),
            P("sku"),
            P(),
        ),
        out_specs=(P("tm", "sku"), P("tm", "sku"), P("tm", "sku"), P("tm", "sku"), P()),
        check_vma=False,
    )
```

```python
import math

import jax
import jax.numpy as jnp
from jax import lax
from jax.experimental import pallas as pl
from jax.experimental.pallas import tpu as pltpu
from jax.sharding import PartitionSpec as P

P_SIZE = 128
LAGMAX = 8
BLOCK = 128
ROWS = 8
F32 = jnp.float32
VMEM = pl.BlockSpec(memory_space=pltpu.VMEM)
SMEM = pl.BlockSpec(memory_space=pltpu.SMEM)


def shifted(value, axis, steps):
    count = lax.axis_size(axis)
    return lax.ppermute(value, axis, [(i, (i + steps) % count) for i in range(count)])


def swapped(value, axis, first):
    count = lax.axis_size(axis)
    pairs = [(i, (i + 1 if (i - first) % 2 == 0 else i - 1) % count) for i in range(count)]
    return lax.ppermute(value, axis, pairs)


def spread(value, axis):
    return lax.all_to_all(value, axis, 0, 0, tiled=True)


def spread_rows(value):
    times, skus = lax.axis_size("tm"), lax.axis_size("sku")
    half = skus // 2
    groups = [
        [t * skus + (side ^ (t // 2 % 4 < 2)) * half + rest for t in range(times)]
        for side in range(2)
        for rest in range(half)
    ]
    return lax.all_to_all(value, ("tm", "sku"), 0, 0, axis_index_groups=groups, tiled=True)


def shape(*dims):
    return jax.ShapeDtypeStruct(dims, F32)


def near(*dims, dtype=F32):
    return pltpu.VMEM(dims, dtype)


def call(kernel, out_shape, operands, smem=0, name=None, grant=16):
    outs = out_shape if isinstance(out_shape, tuple) else (out_shape,)
    size = sum(4 * math.prod(o.shape) for o in (*operands, *outs))
    return pl.pallas_call(
        kernel,
        out_shape=out_shape,
        in_specs=[SMEM] * smem + [VMEM] * (len(operands) - smem),
        out_specs=(VMEM,) * len(out_shape) if isinstance(out_shape, tuple) else VMEM,
        cost_estimate=pl.CostEstimate(flops=20 * size, bytes_accessed=size, transcendentals=0),
        name=name,
        compiler_params=pltpu.CompilerParams(vmem_limit_bytes=grant * 2**20),
    )(*operands)


def step_size(codes, index):
    return 0.05 * (codes[index].astype(F32) + 2.0)


def row_ids():
    return lax.broadcasted_iota(jnp.int32, (ROWS, BLOCK), 0)


def wide(row):
    return jnp.broadcast_to(row, (ROWS, BLOCK))


def ahead(own, after, lag, rows):
    return pltpu.roll(jnp.where(rows >= lag, own, after), ROWS - lag, 0)


def past(own, before, lag, rows):
    return pltpu.roll(jnp.where(rows < ROWS - lag, own, before), lag & (ROWS - 1), 0)


def row_after(own, last, rows):
    return jnp.where(rows == ROWS - 1, last, pltpu.roll(own, ROWS - 1, 0))


def row_before(own, first, rows):
    return jnp.where(rows == 0, first, pltpu.roll(own, 1, 0))


def stock_step(stock, cost, dual, dual_after, primal):
    return jnp.maximum(stock - primal * (cost - dual + dual_after), 0.0)


def price_of(prices, plant_row):
    return jnp.take_along_axis(prices, wide(plant_row), axis=1, mode="promise_in_bounds")


def load_terms(values, plant_row, plant_ids):
    high = values.astype(jnp.bfloat16).astype(F32)
    rest = values - high
    middle = rest.astype(jnp.bfloat16).astype(F32)
    pieces = jnp.concatenate([high, middle, rest - middle], 0).astype(jnp.bfloat16)
    table = jnp.where(plant_ids == plant_row, 1.0, 0.0).astype(jnp.bfloat16)
    return lax.dot_general(table, pieces, (((1,), (1,)), ((), ())), preferred_element_type=F32)


def folded(total):
    total = total.T
    return total[0:8] + total[8:16] + total[16:24]


def blocks(width):
    return [(i, pl.ds(i * BLOCK, BLOCK)) for i in range(width // BLOCK)]


def extra_slot(index, width, slot):
    each = width // ROWS // BLOCK
    start = width + slot * (width // ROWS) + (index % each) * BLOCK
    return slice(index // each, index // each + 1), slice(start, start + BLOCK)


def start(codes, plant_dual, y, v, d, holding, copies):
    rows, width = y.shape
    each = plant_dual.shape[1]
    operands = (codes, plant_dual, y, v, d, holding)
    parts = 4

    def kernel(at_hbm, w, y, v, d, holding, payload, sent, codes, mine, firsts, filled, sems):
        piece = width // parts
        fetches = [
            pltpu.make_async_copy(w, mine, sems.at[0]),
            pltpu.make_async_copy(v.at[0:1], firsts.at[0], sems.at[1]),
            pltpu.make_async_copy(d.at[0:1], firsts.at[1], sems.at[2]),
            pltpu.make_async_copy(holding, firsts.at[2], sems.at[3]),
            pltpu.make_async_copy(at_hbm, codes, sems.at[5 + parts]),
        ]
        for k in range(parts):
            at = pl.ds(k * piece, piece)
            fetches.append(pltpu.make_async_copy(y.at[:, at], sent.at[:, at], sems.at[4 + k]))
        for fetch in fetches:
            fetch.start()
        filled[...] = jnp.zeros(filled.shape, F32)
        fetches[0].wait()
        filled[:, 0:rows, 0:each] = jnp.broadcast_to(mine[...][None], (copies, rows, each))
        out = pltpu.make_async_copy(filled, payload, sems.at[4 + parts])
        out.start()
        for fetch in fetches[1:]:
            fetch.wait()
        primal = step_size(codes, 0)
        for i, at in blocks(width):
            v0, d0, cost = (firsts[k, :, at] for k in range(3))
            stock = stock_step(v0, cost, sent[0:1, at], sent[1:2, at], primal)
            sent[extra_slot(i, width, 0)] = v0 - 2.0 * stock - d0
        out.wait()

    return pl.pallas_call(
        kernel,
        out_shape=(shape(copies, rows, P_SIZE), near(rows, width + width // rows)),
        in_specs=[pl.BlockSpec(memory_space=pltpu.HBM)] * 6,
        out_specs=(pl.BlockSpec(memory_space=pltpu.HBM), VMEM),
        scratch_shapes=[
            pltpu.SMEM(codes.shape, jnp.int32),
            pltpu.VMEM((rows, each), F32),
            pltpu.VMEM((3, 1, width), F32),
            pltpu.VMEM((copies, rows, P_SIZE), F32),
            pltpu.SemaphoreType.DMA((6 + parts,)),
        ],
        name="start",
        compiler_params=pltpu.CompilerParams(vmem_limit_bytes=16 * 2**20),
    )(*(pltpu.with_memory_space_constraint(o, pltpu.HBM) for o in operands))


def stage(scalars, v, d, others):
    operands = (*scalars, v, d, *others)
    count, at_v = len(operands), len(scalars)

    def kernel(*refs):
        outs, (sent, steps, sems) = refs[count : 2 * count], refs[2 * count :]
        copies = [
            pltpu.make_async_copy(refs[i], outs[i] if i > 0 else steps, sems.at[i])
            for i in range(count)
        ]
        for copy in copies:
            copy.start()
        for copy in copies:
            copy.wait()
        outs[0][0], outs[0][1] = steps[0], steps[1]
        outs[0][2] = lax.axis_index("tm") % 2
        v, d = outs[at_v], outs[at_v + 1]
        width = v.shape[1]
        sent[:, 0:width] = v[...]
        for i, at in blocks(width):
            sent[extra_slot(i, width, 0)] = d[0:1, at]
            sent[extra_slot(i, width, 1)] = d[1:2, at]

    width = v.shape[1]
    return pl.pallas_call(
        kernel,
        out_shape=(pltpu.SMEM((3,), jnp.int32),)
        + tuple(pltpu.SMEM(o.shape, o.dtype) for o in scalars[1:])
        + tuple(near(*o.shape, dtype=o.dtype) for o in operands[at_v:])
        + (near(ROWS, width + 2 * (width // ROWS)),),
        in_specs=[pl.BlockSpec(memory_space=pltpu.HBM)] * count,
        out_specs=(SMEM,) * at_v + (VMEM,) * (count - at_v + 1),
        scratch_shapes=[
            pltpu.SMEM(scalars[0].shape, jnp.int32), pltpu.SemaphoreType.DMA((count,)),
        ],
        name="stage",
        compiler_params=pltpu.CompilerParams(vmem_limit_bytes=16 * 2**20),
    )(*(pltpu.with_memory_space_constraint(o, pltpu.HBM) for o in operands))


def first_kernel(
    codes, lags, gathered, x, y, y_next, v, d, cost, holding, load, plants,
    x1, inner, outer, loads, prices,
):
    primal = step_size(codes, 0)
    rows = row_ids()
    plant_ids = lax.broadcasted_iota(jnp.int32, (P_SIZE, BLOCK), 0)
    odd = codes[2] == 1
    width = x.shape[1]
    each = P_SIZE // gathered.shape[0]
    for j in range(gathered.shape[0]):
        prices[:, j * each : (j + 1) * each] = gathered[j, 0:ROWS, 0:each]
    w = prices[...]
    total = jnp.zeros((P_SIZE, 3 * ROWS), F32)
    for i, at in blocks(width):
        lag = lags[i]
        yb = y_next[:, at]
        dual = ahead(y[:, at], yb, lag, rows)
        old = x[:, at]
        charged = price_of(w, plants[:, at]) * load[:, at]
        new = jnp.maximum(old - primal * (cost[:, at] + dual + charged), 0.0)
        over = 2.0 * new - old
        x1[:, at] = new
        total += load_terms(over * load[:, at], plants[:, at], plant_ids)
        v7 = v[7:8, at]
        bar7 = 2.0 * stock_step(v7, holding[:, at], y[7:8, at], yb[0:1], primal) - v7
        field8 = y_next[extra_slot(i, width, 0)] + bar7
        first_row = over[0:1] + jnp.where(lag == LAGMAX, field8, 0.0)
        down = jnp.where(rows == 0, first_row, jnp.where(rows == 1, yb[0:1], d[:, at]))
        inner[:, at] = jnp.where(odd, down, over)
        outer[:, at] = jnp.where(odd, over, down)
        inner[extra_slot(i, width, 0)] = bar7
        outer[extra_slot(i, width, 0)] = bar7
    loads[...] = jnp.broadcast_to(folded(total)[None], loads.shape)


def middle_kernel(
    codes, lags, x, x1, inner, outer, y, y_next, v, v_next, d, holding,
    v2, dual_x, field_x,
):
    primal = step_size(codes, 0)
    dual_step = step_size(codes, 1)
    rows = row_ids()
    odd = codes[2] == 1
    width = v.shape[1]
    square = jnp.zeros((ROWS, BLOCK), F32)
    for i, at in blocks(width):
        lag = lags[i]
        cost = holding[:, at]
        ya, yb = y[:, at], y_next[:, at]
        va, vb = v[:, at], v_next[:, at]
        pair = inner[:, at], outer[:, at]
        bar_prev, mixed = jnp.where(odd, *pair), jnp.where(odd, *pair[::-1])
        da = d[:, at]
        d8, d9 = v_next[extra_slot(i, width, 0)], v_next[extra_slot(i, width, 1)]
        bar8, y16 = mixed[0:1], mixed[1:2]
        db = jnp.where(rows == 0, d8, jnp.where(rows == 1, d9, mixed))
        slot = extra_slot(i, width, 0)
        bar_before = jnp.where(odd, inner[slot], outer[slot])
        over = 2.0 * x1[:, at] - x[:, at]
        va1 = stock_step(va, cost, ya, row_after(ya, yb[0:1], rows), primal)
        vb1 = stock_step(vb, cost, yb, row_after(yb, y16, rows), primal)
        va_bar = 2.0 * va1 - va
        vb_bar = 2.0 * vb1 - vb
        ha = -da - va_bar + row_before(va_bar, bar_before, rows)
        hb = -db - vb_bar + row_before(vb_bar, va_bar[7:8], rows)
        misfit = ahead(ha, hb, lag, rows) + over
        square += misfit * misfit
        yx = ahead(ya, yb, lag, rows) + dual_step * misfit
        dual_x[:, at] = yx
        ya1 = ya + dual_step * (ha + past(over, bar_prev, lag, rows))
        y8 = yb[0:1] + dual_step * (hb[0:1] + pltpu.roll(over, lag & (ROWS - 1), 0)[0:1])
        va2 = stock_step(va1, cost, ya1, row_after(ya1, y8, rows), primal)
        v2[:, at] = va2
        start_bar = pltpu.roll(2.0 * va2 - va1, (ROWS - lag + 1) & (ROWS - 1), 0)[0:1]
        whole = lag == LAGMAX
        y_end = jnp.where(whole, y16, pltpu.roll(yb, ROWS - lag, 0)[0:1])
        h_end = jnp.where(whole, 0.0, pltpu.roll(hb, ROWS - lag, 0)[0:1])
        yx_end = y_end + dual_step * (h_end + bar8)
        vx1 = ahead(va1, vb1, lag, rows)
        vx2 = stock_step(vx1, cost, yx, row_after(yx, yx_end, rows), primal)
        vx_bar = 2.0 * vx2 - vx1
        dx = ahead(da, db, lag, rows)
        field_x[:, at] = -dx - vx_bar + row_before(vx_bar, start_bar, rows)
    field_x[:, width : width + BLOCK] = square


def second_kernel(
    codes, sums, prices, cap, x, dual, field, cost, load, plants,
    x2, dual_x, loads, prices_new, excess_row,
):
    primal = step_size(codes, 0)
    dual_step = step_size(codes, 1)
    plant_step = dual_step * (P_SIZE / (x.shape[1] * sums.shape[0]))
    plant_ids = lax.broadcasted_iota(jnp.int32, (P_SIZE, BLOCK), 0)
    excess = jnp.sum(sums[...], axis=0) - cap[...]
    w = jnp.maximum(prices[...] + plant_step * excess, 0.0)
    prices_new[...] = w
    above = jnp.maximum(excess, 0.0)
    excess_row[...] = jnp.sum(above * above, axis=0, keepdims=True)
    total = jnp.zeros((P_SIZE, 3 * ROWS), F32)
    square = jnp.zeros((ROWS, BLOCK), F32)
    for i, at in blocks(x.shape[1]):
        old = x[:, at]
        charged = price_of(w, plants[:, at]) * load[:, at]
        new = jnp.maximum(old - primal * (cost[:, at] + dual[:, at] + charged), 0.0)
        over = 2.0 * new - old
        x2[:, at] = new
        misfit = field[:, at] + over
        dual_x[:, at] = dual[:, at] + dual_step * misfit
        square += misfit * misfit
        total += load_terms(over * load[:, at], plants[:, at], plant_ids)
    own = folded(total)
    pair = (field[:, x.shape[1] :], square)
    lines = [own[k : k + 1] for k in range(ROWS)]
    lines += [jnp.sum(p, axis=0, keepdims=True) for p in pair]
    for k, line in enumerate(lines):
        at = slice(k * P_SIZE, (k + 1) * P_SIZE)
        loads[:, :, at] = jnp.broadcast_to(line[None], (loads.shape[0], 1, P_SIZE))


def third_kernel(codes, sums, prices, cap, excess_row, price_out, out, *, total_skus):
    plant_step = step_size(codes, 1) * (P_SIZE / total_skus)
    row = jnp.sum(sums[...], axis=0)
    totals = jnp.concatenate(
        [row[:, k * P_SIZE : (k + 1) * P_SIZE] for k in range(ROWS + 2)], axis=0
    )
    excess = totals[0:8] - cap[...]
    price_out[...] = jnp.maximum(prices[...] + plant_step * excess, 0.0)
    above = jnp.maximum(excess, 0.0)
    above_row = jnp.sum(above * above, axis=0, keepdims=True)
    for k, rows in enumerate(((totals[8:9], excess_row[...]), (totals[9:10], above_row))):
        pair = jnp.concatenate(rows, 0)
        out[:, k] = jnp.broadcast_to(pair[None], (out.shape[0],) + pair.shape)


def unshift_kernel(lags, dual, dual_prev, y):
    rows = row_ids()
    for i, at in blocks(y.shape[1]):
        y[:, at] = past(dual[:, at], dual_prev[:, at], lags[i], rows)


def body(
    primal_x,
    stock_v,
    balance_dual,
    plant_dual,
    demand,
    unit_cost,
    holding_cost,
    load_coef,
    capacity,
    lags,
    plants,
    step_codes,
):
    width = primal_x.shape[1]
    skus = lax.axis_size("sku")
    times = lax.axis_size("tm")
    each = plant_dual.shape[1]
    total_skus = width * skus
    owner = lax.axis_index("sku") * each
    cost = unit_cost.reshape(1, width)
    holding = holding_cost.reshape(1, width)
    load = load_coef.reshape(1, width)
    plant_row = plants.reshape(1, width)

    payload, y_sent = start(
        step_codes, plant_dual, balance_dual, stock_v, demand, holding, skus
    )
    y_next = shifted(y_sent, "tm", -1)
    payload, codes, lags, v, d, *held = lax.optimization_barrier(
        (
            payload, step_codes, lags, stock_v, demand, primal_x, balance_dual, cost, holding,
            load, plant_row, capacity,
        )
    )
    codes, lags, v, d, x, y, cost, holding, load, plant_row, limits, v_sent = stage(
        (codes, lags), v, d, held
    )
    v_next = shifted(v_sent, "tm", -1)
    gathered = spread(payload, "sku")
    x1, inner, outer, loads1, prices0 = call(
        first_kernel,
        (
            near(ROWS, width), near(ROWS, width + width // ROWS),
            near(ROWS, width + width // ROWS), shape(skus, ROWS, P_SIZE), near(ROWS, P_SIZE),
        ),
        (codes, lags, gathered, x, y, y_next, v, d, cost, holding, load, plant_row),
        smem=2,
        name="first",
    )
    inner = swapped(inner, "tm", 0)
    outer = swapped(outer, "tm", 1)
    sums1 = spread(loads1, "sku")
    v2, dual_x, field_x = call(
        middle_kernel,
        (near(ROWS, width), near(ROWS, width), near(ROWS, width + BLOCK)),
        (codes, lags, x, x1, inner, outer, y, y_next, v, v_next, d, holding),
        smem=2,
        name="middle",
    )
    x2, dual_x2, loads2, prices1, above1 = call(
        second_kernel,
        (
            near(ROWS, width), near(ROWS, width), shape(skus, 1, (ROWS + 2) * P_SIZE),
            near(ROWS, P_SIZE), near(1, P_SIZE),
        ),
        (
            codes, sums1, prices0, limits, x1, dual_x, field_x, cost, load,
            plant_row,
        ),
        smem=1,
        name="second",
    )
    sums2 = spread(loads2, "sku")
    dual_prev = shifted(dual_x2, "tm", 1)

    def third(*refs):
        third_kernel(*refs, total_skus=total_skus)

    prices2, packed = call(
        third,
        (near(ROWS, P_SIZE), shape(times, 2, 2, P_SIZE)),
        (codes, sums2, prices1, limits, above1),
        smem=1,
        name="third",
    )
    portion = lax.dynamic_slice_in_dim(prices2, owner, each, 1)
    totals = jnp.sum(spread_rows(packed), axis=(0, 3))
    scale = P_SIZE / total_skus
    cells, cap_rows = ROWS * times * total_skus, ROWS * times * P_SIZE
    column = lax.broadcasted_iota(jnp.int32, totals.shape, 1)
    residuals = totals * jnp.where(column == 0, 1.0 / cells, scale * scale / cap_rows)
    next_y = call(
        unshift_kernel, shape(ROWS, width), (lags, dual_x2, dual_prev), smem=1, name="unshift"
    )
    return x2, v2, next_y, portion, residuals


def solution(mesh):
    return jax.shard_map(
        body,
        mesh=mesh,
        in_specs=(
            P("tm", "sku"),
            P("tm", "sku"),
            P("tm", "sku"),
            P("tm", "sku"),
            P("tm", "sku"),
            P("sku"),
            P("sku"),
            P("sku"),
            P("tm", None),
            P("sku"),
            P("sku"),
            P(),
        ),
        out_specs=(P("tm", "sku"), P("tm", "sku"), P("tm", "sku"), P("tm", "sku"), P()),
        check_vma=False,
    )
```

```python
import math

import jax
import jax.numpy as jnp
from jax import lax
from jax.experimental import pallas as pl
from jax.experimental.pallas import tpu as pltpu
from jax.sharding import PartitionSpec as P

P_SIZE = 128
LAGMAX = 8
BLOCK = 128
ROWS = 8
F32 = jnp.float32
VMEM = pl.BlockSpec(memory_space=pltpu.VMEM)
SMEM = pl.BlockSpec(memory_space=pltpu.SMEM)


def shifted(value, axis, steps):
    count = lax.axis_size(axis)
    return lax.ppermute(value, axis, [(i, (i + steps) % count) for i in range(count)])


def swapped(value, axis, first):
    count = lax.axis_size(axis)
    pairs = [(i, (i + 1 if (i - first) % 2 == 0 else i - 1) % count) for i in range(count)]
    return lax.ppermute(value, axis, pairs)


def spread(value, axis):
    return lax.all_to_all(value, axis, 0, 0, tiled=True)


def spread_rows(value):
    times, skus = lax.axis_size("tm"), lax.axis_size("sku")
    half = skus // 2
    groups = [
        [t * skus + (side ^ (t // 2 % 4 < 2)) * half + rest for t in range(times)]
        for side in range(2)
        for rest in range(half)
    ]
    return lax.all_to_all(value, ("tm", "sku"), 0, 0, axis_index_groups=groups, tiled=True)


def shape(*dims):
    return jax.ShapeDtypeStruct(dims, F32)


def near(*dims, dtype=F32):
    return pltpu.VMEM(dims, dtype)


def call(kernel, out_shape, operands, smem=0, name=None, grant=16):
    outs = out_shape if isinstance(out_shape, tuple) else (out_shape,)
    size = sum(4 * math.prod(o.shape) for o in (*operands, *outs))
    return pl.pallas_call(
        kernel,
        out_shape=out_shape,
        in_specs=[SMEM] * smem + [VMEM] * (len(operands) - smem),
        out_specs=(VMEM,) * len(out_shape) if isinstance(out_shape, tuple) else VMEM,
        cost_estimate=pl.CostEstimate(flops=20 * size, bytes_accessed=size, transcendentals=0),
        name=name,
        compiler_params=pltpu.CompilerParams(vmem_limit_bytes=grant * 2**20),
    )(*operands)


def step_size(codes, index):
    return 0.05 * (codes[index].astype(F32) + 2.0)


def row_ids():
    return lax.broadcasted_iota(jnp.int32, (ROWS, BLOCK), 0)


def wide(row):
    return jnp.broadcast_to(row, (ROWS, BLOCK))


def ahead(own, after, lag, rows):
    return pltpu.roll(jnp.where(rows >= lag, own, after), ROWS - lag, 0)


def past(own, before, lag, rows):
    return pltpu.roll(jnp.where(rows < ROWS - lag, own, before), lag & (ROWS - 1), 0)


def row_after(own, last, rows):
    return jnp.where(rows == ROWS - 1, last, pltpu.roll(own, ROWS - 1, 0))


def row_before(own, first, rows):
    return jnp.where(rows == 0, first, pltpu.roll(own, 1, 0))


def stock_step(stock, cost, dual, dual_after, primal):
    return jnp.maximum(stock - primal * (cost - dual + dual_after), 0.0)


def price_of(prices, plant_row):
    return jnp.take_along_axis(prices, wide(plant_row), axis=1, mode="promise_in_bounds")


def load_terms(values, plant_row, plant_ids):
    high = values.astype(jnp.bfloat16).astype(F32)
    rest = values - high
    middle = rest.astype(jnp.bfloat16).astype(F32)
    pieces = jnp.concatenate([high, middle, rest - middle], 0).astype(jnp.bfloat16)
    table = jnp.where(plant_ids == plant_row, 1.0, 0.0).astype(jnp.bfloat16)
    return lax.dot_general(table, pieces, (((1,), (1,)), ((), ())), preferred_element_type=F32)


def folded(total):
    total = total.T
    return total[0:8] + total[8:16] + total[16:24]


def blocks(width):
    return [(i, pl.ds(i * BLOCK, BLOCK)) for i in range(width // BLOCK)]


def extra_slot(index, width, slot):
    each = width // ROWS // BLOCK
    start = width + slot * (width // ROWS) + (index % each) * BLOCK
    return slice(index // each, index // each + 1), slice(start, start + BLOCK)


def start(codes, plant_dual, y, v, d, holding, copies):
    rows, width = y.shape
    each = plant_dual.shape[1]
    operands = (codes, plant_dual, y, v, d, holding)
    parts = 4

    def kernel(at_hbm, w, y, v, d, holding, payload, sent, codes, mine, firsts, filled, sems):
        piece = width // parts
        fetches = [
            pltpu.make_async_copy(w, mine, sems.at[0]),
            pltpu.make_async_copy(v.at[0:1], firsts.at[0], sems.at[1]),
            pltpu.make_async_copy(d.at[0:1], firsts.at[1], sems.at[2]),
            pltpu.make_async_copy(holding, firsts.at[2], sems.at[3]),
            pltpu.make_async_copy(at_hbm, codes, sems.at[5 + parts]),
        ]
        for k in range(parts):
            at = pl.ds(k * piece, piece)
            fetches.append(pltpu.make_async_copy(y.at[:, at], sent.at[:, at], sems.at[4 + k]))
        for fetch in fetches:
            fetch.start()
        filled[...] = jnp.zeros(filled.shape, F32)
        fetches[0].wait()
        filled[:, 0:rows, 0:each] = jnp.broadcast_to(mine[...][None], (copies, rows, each))
        out = pltpu.make_async_copy(filled, payload, sems.at[4 + parts])
        out.start()
        for fetch in fetches[1:]:
            fetch.wait()
        primal = step_size(codes, 0)
        for i, at in blocks(width):
            v0, d0, cost = (firsts[k, :, at] for k in range(3))
            stock = stock_step(v0, cost, sent[0:1, at], sent[1:2, at], primal)
            sent[extra_slot(i, width, 0)] = v0 - 2.0 * stock - d0
        out.wait()

    return pl.pallas_call(
        kernel,
        out_shape=(shape(copies, rows, P_SIZE), near(rows, width + width // rows)),
        in_specs=[pl.BlockSpec(memory_space=pltpu.HBM)] * 6,
        out_specs=(pl.BlockSpec(memory_space=pltpu.HBM), VMEM),
        scratch_shapes=[
            pltpu.SMEM(codes.shape, jnp.int32),
            pltpu.VMEM((rows, each), F32),
            pltpu.VMEM((3, 1, width), F32),
            pltpu.VMEM((copies, rows, P_SIZE), F32),
            pltpu.SemaphoreType.DMA((6 + parts,)),
        ],
        name="start",
        compiler_params=pltpu.CompilerParams(vmem_limit_bytes=16 * 2**20),
    )(*(pltpu.with_memory_space_constraint(o, pltpu.HBM) for o in operands))


def stage(scalars, v, d, others):
    operands = (*scalars, v, d, *others)
    count, at_v = len(operands), len(scalars)

    def kernel(*refs):
        outs, (sent, steps, sems) = refs[count : 2 * count], refs[2 * count :]
        copies = [
            pltpu.make_async_copy(refs[i], outs[i] if i > 0 else steps, sems.at[i])
            for i in range(count)
        ]
        for copy in copies:
            copy.start()
        for copy in copies:
            copy.wait()
        outs[0][0], outs[0][1] = steps[0], steps[1]
        outs[0][2] = lax.axis_index("tm") % 2
        v, d = outs[at_v], outs[at_v + 1]
        width = v.shape[1]
        sent[:, 0:width] = v[...]
        for i, at in blocks(width):
            sent[extra_slot(i, width, 0)] = d[0:1, at]
            sent[extra_slot(i, width, 1)] = d[1:2, at]

    width = v.shape[1]
    return pl.pallas_call(
        kernel,
        out_shape=(pltpu.SMEM((3,), jnp.int32),)
        + tuple(pltpu.SMEM(o.shape, o.dtype) for o in scalars[1:])
        + tuple(near(*o.shape, dtype=o.dtype) for o in operands[at_v:])
        + (near(ROWS, width + 2 * (width // ROWS)),),
        in_specs=[pl.BlockSpec(memory_space=pltpu.HBM)] * count,
        out_specs=(SMEM,) * at_v + (VMEM,) * (count - at_v + 1),
        scratch_shapes=[
            pltpu.SMEM(scalars[0].shape, jnp.int32), pltpu.SemaphoreType.DMA((count,)),
        ],
        name="stage",
        compiler_params=pltpu.CompilerParams(vmem_limit_bytes=16 * 2**20),
    )(*(pltpu.with_memory_space_constraint(o, pltpu.HBM) for o in operands))


def first_kernel(
    codes, lags, gathered, x, y, y_next, v, d, cost, holding, load, plants,
    x1, inner, outer, loads, prices,
):
    primal = step_size(codes, 0)
    rows = row_ids()
    plant_ids = lax.broadcasted_iota(jnp.int32, (P_SIZE, BLOCK), 0)
    odd = codes[2] == 1
    width = x.shape[1]
    each = P_SIZE // gathered.shape[0]
    for j in range(gathered.shape[0]):
        prices[:, j * each : (j + 1) * each] = gathered[j, 0:ROWS, 0:each]
    w = prices[...]
    total = jnp.zeros((P_SIZE, 3 * ROWS), F32)
    for i, at in blocks(width):
        lag = lags[i]
        yb = y_next[:, at]
        dual = ahead(y[:, at], yb, lag, rows)
        old = x[:, at]
        charged = price_of(w, plants[:, at]) * load[:, at]
        new = jnp.maximum(old - primal * (cost[:, at] + dual + charged), 0.0)
        over = 2.0 * new - old
        x1[:, at] = new
        total += load_terms(over * load[:, at], plants[:, at], plant_ids)
        v7 = v[7:8, at]
        bar7 = 2.0 * stock_step(v7, holding[:, at], y[7:8, at], yb[0:1], primal) - v7
        field8 = y_next[extra_slot(i, width, 0)] + bar7
        first_row = over[0:1] + jnp.where(lag == LAGMAX, field8, 0.0)
        down = jnp.where(rows == 0, first_row, jnp.where(rows == 1, yb[0:1], d[:, at]))
        up = over + jnp.where(rows == ROWS - lag, bar7, 0.0)
        inner[:, at] = jnp.where(odd, down, up)
        outer[:, at] = jnp.where(odd, up, down)
    loads[...] = jnp.broadcast_to(folded(total)[None], loads.shape)


def middle_kernel(
    codes, lags, x, x1, inner, outer, y, y_next, v, v_next, d, holding,
    v2, dual_x, field_x,
):
    primal = step_size(codes, 0)
    dual_step = step_size(codes, 1)
    rows = row_ids()
    odd = codes[2] == 1
    width = v.shape[1]
    square = jnp.zeros((ROWS, BLOCK), F32)
    for i, at in blocks(width):
        lag = lags[i]
        cost = holding[:, at]
        ya, yb = y[:, at], y_next[:, at]
        va, vb = v[:, at], v_next[:, at]
        pair = inner[:, at], outer[:, at]
        bar_prev, mixed = jnp.where(odd, *pair), jnp.where(odd, *pair[::-1])
        da = d[:, at]
        d8, d9 = v_next[extra_slot(i, width, 0)], v_next[extra_slot(i, width, 1)]
        bar8, y16 = mixed[0:1], mixed[1:2]
        db = jnp.where(rows == 0, d8, jnp.where(rows == 1, d9, mixed))
        over = 2.0 * x1[:, at] - x[:, at]
        va1 = stock_step(va, cost, ya, row_after(ya, yb[0:1], rows), primal)
        vb1 = stock_step(vb, cost, yb, row_after(yb, y16, rows), primal)
        va_bar = 2.0 * va1 - va
        vb_bar = 2.0 * vb1 - vb
        ha = -da - va_bar + row_before(va_bar, jnp.zeros((1, BLOCK), F32), rows)
        hb = -db - vb_bar + row_before(vb_bar, va_bar[7:8], rows)
        misfit = ahead(ha, hb, lag, rows) + over
        square += misfit * misfit
        yx = ahead(ya, yb, lag, rows) + dual_step * misfit
        dual_x[:, at] = yx
        ya1 = ya + dual_step * (ha + past(over, bar_prev, lag, rows))
        y8 = yb[0:1] + dual_step * (hb[0:1] + pltpu.roll(over, lag & (ROWS - 1), 0)[0:1])
        va2 = stock_step(va1, cost, ya1, row_after(ya1, y8, rows), primal)
        v2[:, at] = va2
        start_bar = pltpu.roll(2.0 * va2 - va1, (ROWS - lag + 1) & (ROWS - 1), 0)[0:1]
        whole = lag == LAGMAX
        y_end = jnp.where(whole, y16, pltpu.roll(yb, ROWS - lag, 0)[0:1])
        h_end = jnp.where(whole, 0.0, pltpu.roll(hb, ROWS - lag, 0)[0:1])
        yx_end = y_end + dual_step * (h_end + bar8)
        vx1 = ahead(va1, vb1, lag, rows)
        vx2 = stock_step(vx1, cost, yx, row_after(yx, yx_end, rows), primal)
        vx_bar = 2.0 * vx2 - vx1
        dx = ahead(da, db, lag, rows)
        field_x[:, at] = -dx - vx_bar + row_before(vx_bar, start_bar, rows)
    field_x[:, width : width + BLOCK] = square


def second_kernel(
    codes, sums, prices, cap, x, dual, field, cost, load, plants,
    x2, dual_x, loads, prices_new, excess_row,
):
    primal = step_size(codes, 0)
    dual_step = step_size(codes, 1)
    plant_step = dual_step * (P_SIZE / (x.shape[1] * sums.shape[0]))
    plant_ids = lax.broadcasted_iota(jnp.int32, (P_SIZE, BLOCK), 0)
    excess = jnp.sum(sums[...], axis=0) - cap[...]
    w = jnp.maximum(prices[...] + plant_step * excess, 0.0)
    prices_new[...] = w
    above = jnp.maximum(excess, 0.0)
    excess_row[...] = jnp.sum(above * above, axis=0, keepdims=True)
    total = jnp.zeros((P_SIZE, 3 * ROWS), F32)
    square = jnp.zeros((ROWS, BLOCK), F32)
    for i, at in blocks(x.shape[1]):
        old = x[:, at]
        charged = price_of(w, plants[:, at]) * load[:, at]
        new = jnp.maximum(old - primal * (cost[:, at] + dual[:, at] + charged), 0.0)
        over = 2.0 * new - old
        x2[:, at] = new
        misfit = field[:, at] + over
        dual_x[:, at] = dual[:, at] + dual_step * misfit
        square += misfit * misfit
        total += load_terms(over * load[:, at], plants[:, at], plant_ids)
    own = folded(total)
    pair = (field[:, x.shape[1] :], square)
    lines = [own[k : k + 1] for k in range(ROWS)]
    lines += [jnp.sum(p, axis=0, keepdims=True) for p in pair]
    for k, line in enumerate(lines):
        at = slice(k * P_SIZE, (k + 1) * P_SIZE)
        loads[:, :, at] = jnp.broadcast_to(line[None], (loads.shape[0], 1, P_SIZE))


def third_kernel(codes, sums, prices, cap, excess_row, price_out, out, *, total_skus):
    plant_step = step_size(codes, 1) * (P_SIZE / total_skus)
    row = jnp.sum(sums[...], axis=0)
    totals = jnp.concatenate(
        [row[:, k * P_SIZE : (k + 1) * P_SIZE] for k in range(ROWS + 2)], axis=0
    )
    excess = totals[0:8] - cap[...]
    price_out[...] = jnp.maximum(prices[...] + plant_step * excess, 0.0)
    above = jnp.maximum(excess, 0.0)
    above_row = jnp.sum(above * above, axis=0, keepdims=True)
    for k, rows in enumerate(((totals[8:9], excess_row[...]), (totals[9:10], above_row))):
        pair = jnp.concatenate(rows, 0)
        out[:, k] = jnp.broadcast_to(pair[None], (out.shape[0],) + pair.shape)


def unshift_kernel(lags, dual, dual_prev, y):
    rows = row_ids()
    for i, at in blocks(y.shape[1]):
        y[:, at] = past(dual[:, at], dual_prev[:, at], lags[i], rows)


def body(
    primal_x,
    stock_v,
    balance_dual,
    plant_dual,
    demand,
    unit_cost,
    holding_cost,
    load_coef,
    capacity,
    lags,
    plants,
    step_codes,
):
    width = primal_x.shape[1]
    skus = lax.axis_size("sku")
    times = lax.axis_size("tm")
    each = plant_dual.shape[1]
    total_skus = width * skus
    owner = lax.axis_index("sku") * each
    cost = unit_cost.reshape(1, width)
    holding = holding_cost.reshape(1, width)
    load = load_coef.reshape(1, width)
    plant_row = plants.reshape(1, width)

    payload, y_sent = start(
        step_codes, plant_dual, balance_dual, stock_v, demand, holding, skus
    )
    y_next = shifted(y_sent, "tm", -1)
    payload, codes, lags, v, d, *held = lax.optimization_barrier(
        (
            payload, step_codes, lags, stock_v, demand, primal_x, balance_dual, cost, holding,
            load, plant_row, capacity,
        )
    )
    codes, lags, v, d, x, y, cost, holding, load, plant_row, limits, v_sent = stage(
        (codes, lags), v, d, held
    )
    v_next = shifted(v_sent, "tm", -1)
    gathered = spread(payload, "sku")
    x1, inner, outer, loads1, prices0 = call(
        first_kernel,
        (
            near(ROWS, width), near(ROWS, width), near(ROWS, width),
            shape(skus, ROWS, P_SIZE), near(ROWS, P_SIZE),
        ),
        (codes, lags, gathered, x, y, y_next, v, d, cost, holding, load, plant_row),
        smem=2,
        name="first",
    )
    inner = swapped(inner, "tm", 0)
    outer = swapped(outer, "tm", 1)
    sums1 = spread(loads1, "sku")
    v2, dual_x, field_x = call(
        middle_kernel,
        (near(ROWS, width), near(ROWS, width), near(ROWS, width + BLOCK)),
        (codes, lags, x, x1, inner, outer, y, y_next, v, v_next, d, holding),
        smem=2,
        name="middle",
    )
    x2, dual_x2, loads2, prices1, above1 = call(
        second_kernel,
        (
            near(ROWS, width), near(ROWS, width), shape(skus, 1, (ROWS + 2) * P_SIZE),
            near(ROWS, P_SIZE), near(1, P_SIZE),
        ),
        (
            codes, sums1, prices0, limits, x1, dual_x, field_x, cost, load,
            plant_row,
        ),
        smem=1,
        name="second",
    )
    sums2 = spread(loads2, "sku")
    dual_prev = shifted(dual_x2, "tm", 1)

    def third(*refs):
        third_kernel(*refs, total_skus=total_skus)

    prices2, packed = call(
        third,
        (near(ROWS, P_SIZE), shape(times, 2, 2, P_SIZE)),
        (codes, sums2, prices1, limits, above1),
        smem=1,
        name="third",
    )
    portion = lax.dynamic_slice_in_dim(prices2, owner, each, 1)
    totals = jnp.sum(spread_rows(packed), axis=(0, 3))
    scale = P_SIZE / total_skus
    cells, cap_rows = ROWS * times * total_skus, ROWS * times * P_SIZE
    column = lax.broadcasted_iota(jnp.int32, totals.shape, 1)
    residuals = totals * jnp.where(column == 0, 1.0 / cells, scale * scale / cap_rows)
    next_y = call(
        unshift_kernel, shape(ROWS, width), (lags, dual_x2, dual_prev), smem=1, name="unshift"
    )
    return x2, v2, next_y, portion, residuals


def solution(mesh):
    return jax.shard_map(
        body,
        mesh=mesh,
        in_specs=(
            P("tm", "sku"),
            P("tm", "sku"),
            P("tm", "sku"),
            P("tm", "sku"),
            P("tm", "sku"),
            P("sku"),
            P("sku"),
            P("sku"),
            P("tm", None),
            P("sku"),
            P("sku"),
            P(),
        ),
        out_specs=(P("tm", "sku"), P("tm", "sku"), P("tm", "sku"), P("tm", "sku"), P()),
        check_vma=False,
    )
```

```python
import math

import jax
import jax.numpy as jnp
from jax import lax
from jax.experimental import pallas as pl
from jax.experimental.pallas import tpu as pltpu
from jax.sharding import PartitionSpec as P

P_SIZE = 128
LAGMAX = 8
BLOCK = 128
ROWS = 8
F32 = jnp.float32
VMEM = pl.BlockSpec(memory_space=pltpu.VMEM)
SMEM = pl.BlockSpec(memory_space=pltpu.SMEM)


def shifted(value, axis, steps):
    count = lax.axis_size(axis)
    return lax.ppermute(value, axis, [(i, (i + steps) % count) for i in range(count)])


def swapped(value, axis, first):
    count = lax.axis_size(axis)
    pairs = [(i, (i + 1 if (i - first) % 2 == 0 else i - 1) % count) for i in range(count)]
    return lax.ppermute(value, axis, pairs)


def spread(value, axis):
    return lax.all_to_all(value, axis, 0, 0, tiled=True)


def spread_rows(value):
    times, skus = lax.axis_size("tm"), lax.axis_size("sku")
    half = skus // 2
    groups = [
        [t * skus + (side ^ (t // 2 % 4 < 2)) * half + rest for t in range(times)]
        for side in range(2)
        for rest in range(half)
    ]
    return lax.all_to_all(value, ("tm", "sku"), 0, 0, axis_index_groups=groups, tiled=True)


def shape(*dims):
    return jax.ShapeDtypeStruct(dims, F32)


def near(*dims, dtype=F32):
    return pltpu.VMEM(dims, dtype)


def call(kernel, out_shape, operands, smem=0, name=None, grant=16):
    outs = out_shape if isinstance(out_shape, tuple) else (out_shape,)
    size = sum(4 * math.prod(o.shape) for o in (*operands, *outs))
    return pl.pallas_call(
        kernel,
        out_shape=out_shape,
        in_specs=[SMEM] * smem + [VMEM] * (len(operands) - smem),
        out_specs=(VMEM,) * len(out_shape) if isinstance(out_shape, tuple) else VMEM,
        cost_estimate=pl.CostEstimate(flops=20 * size, bytes_accessed=size, transcendentals=0),
        name=name,
        compiler_params=pltpu.CompilerParams(vmem_limit_bytes=grant * 2**20),
    )(*operands)


def step_size(codes, index):
    return 0.05 * (codes[index].astype(F32) + 2.0)


def row_ids():
    return lax.broadcasted_iota(jnp.int32, (ROWS, BLOCK), 0)


def wide(row):
    return jnp.broadcast_to(row, (ROWS, BLOCK))


def ahead(own, after, lag, rows):
    return pltpu.roll(jnp.where(rows >= lag, own, after), ROWS - lag, 0)


def past(own, before, lag, rows):
    return pltpu.roll(jnp.where(rows < ROWS - lag, own, before), lag & (ROWS - 1), 0)


def row_after(own, last, rows):
    return jnp.where(rows == ROWS - 1, last, pltpu.roll(own, ROWS - 1, 0))


def row_before(own, first, rows):
    return jnp.where(rows == 0, first, pltpu.roll(own, 1, 0))


def stock_step(stock, cost, dual, dual_after, primal):
    return jnp.maximum(stock - primal * (cost - dual + dual_after), 0.0)


def price_of(prices, plant_row):
    return jnp.take_along_axis(prices, wide(plant_row), axis=1, mode="promise_in_bounds")


def load_terms(values, plant_row, plant_ids):
    high = values.astype(jnp.bfloat16).astype(F32)
    rest = values - high
    middle = rest.astype(jnp.bfloat16).astype(F32)
    pieces = jnp.concatenate([high, middle, rest - middle], 0).astype(jnp.bfloat16)
    table = jnp.where(plant_ids == plant_row, 1.0, 0.0).astype(jnp.bfloat16)
    return lax.dot_general(table, pieces, (((1,), (1,)), ((), ())), preferred_element_type=F32)


def folded(total):
    total = total.T
    return total[0:8] + total[8:16] + total[16:24]


def blocks(width):
    return [(i, pl.ds(i * BLOCK, BLOCK)) for i in range(width // BLOCK)]


def extra_slot(index, width, slot):
    each = width // ROWS // BLOCK
    start = width + slot * (width // ROWS) + (index % each) * BLOCK
    return slice(index // each, index // each + 1), slice(start, start + BLOCK)


def start(codes, plant_dual, y, v, d, holding, copies):
    rows, width = y.shape
    each = plant_dual.shape[1]
    operands = (codes, plant_dual, y, v, d, holding)
    parts = 4

    def kernel(at_hbm, w, y, v, d, holding, payload, sent, codes, mine, firsts, filled, sems):
        piece = width // parts
        fetches = [
            pltpu.make_async_copy(w, mine, sems.at[0]),
            pltpu.make_async_copy(v.at[0:1], firsts.at[0], sems.at[1]),
            pltpu.make_async_copy(d.at[0:1], firsts.at[1], sems.at[2]),
            pltpu.make_async_copy(holding, firsts.at[2], sems.at[3]),
            pltpu.make_async_copy(at_hbm, codes, sems.at[5 + parts]),
        ]
        for k in range(parts):
            at = pl.ds(k * piece, piece)
            fetches.append(pltpu.make_async_copy(y.at[:, at], sent.at[:, at], sems.at[4 + k]))
        for fetch in fetches:
            fetch.start()
        filled[...] = jnp.zeros(filled.shape, F32)
        fetches[0].wait()
        filled[:, 0:rows, 0:each] = jnp.broadcast_to(mine[...][None], (copies, rows, each))
        out = pltpu.make_async_copy(filled, payload, sems.at[4 + parts])
        out.start()
        for fetch in fetches[1:]:
            fetch.wait()
        primal = step_size(codes, 0)
        for i, at in blocks(width):
            v0, d0, cost = (firsts[k, :, at] for k in range(3))
            stock = stock_step(v0, cost, sent[0:1, at], sent[1:2, at], primal)
            sent[extra_slot(i, width, 0)] = v0 - 2.0 * stock - d0
        out.wait()

    return pl.pallas_call(
        kernel,
        out_shape=(shape(copies, rows, P_SIZE), near(rows, width + width // rows)),
        in_specs=[pl.BlockSpec(memory_space=pltpu.HBM)] * 6,
        out_specs=(pl.BlockSpec(memory_space=pltpu.HBM), VMEM),
        scratch_shapes=[
            pltpu.SMEM(codes.shape, jnp.int32),
            pltpu.VMEM((rows, each), F32),
            pltpu.VMEM((3, 1, width), F32),
            pltpu.VMEM((copies, rows, P_SIZE), F32),
            pltpu.SemaphoreType.DMA((6 + parts,)),
        ],
        name="start",
        compiler_params=pltpu.CompilerParams(vmem_limit_bytes=16 * 2**20),
    )(*(pltpu.with_memory_space_constraint(o, pltpu.HBM) for o in operands))


def stage(scalars, v, d, others):
    operands = (*scalars, v, d, *others)
    count, at_v = len(operands), len(scalars)

    def kernel(*refs):
        outs, (sent, steps, sems) = refs[count : 2 * count], refs[2 * count :]
        copies = [
            pltpu.make_async_copy(refs[i], outs[i] if i > 0 else steps, sems.at[i])
            for i in range(count)
        ]
        for copy in copies:
            copy.start()
        for copy in copies:
            copy.wait()
        outs[0][0], outs[0][1] = steps[0], steps[1]
        outs[0][2] = lax.axis_index("tm") % 2
        v, d = outs[at_v], outs[at_v + 1]
        width = v.shape[1]
        sent[:, 0:width] = v[...]
        for i, at in blocks(width):
            sent[extra_slot(i, width, 0)] = d[0:1, at]
            sent[extra_slot(i, width, 1)] = d[1:2, at]

    width = v.shape[1]
    return pl.pallas_call(
        kernel,
        out_shape=(pltpu.SMEM((3,), jnp.int32),)
        + tuple(pltpu.SMEM(o.shape, o.dtype) for o in scalars[1:])
        + tuple(near(*o.shape, dtype=o.dtype) for o in operands[at_v:])
        + (near(ROWS, width + 2 * (width // ROWS)),),
        in_specs=[pl.BlockSpec(memory_space=pltpu.HBM)] * count,
        out_specs=(SMEM,) * at_v + (VMEM,) * (count - at_v + 1),
        scratch_shapes=[
            pltpu.SMEM(scalars[0].shape, jnp.int32), pltpu.SemaphoreType.DMA((count,)),
        ],
        name="stage",
        compiler_params=pltpu.CompilerParams(vmem_limit_bytes=16 * 2**20),
    )(*(pltpu.with_memory_space_constraint(o, pltpu.HBM) for o in operands))


def first_kernel(
    codes, lags, gathered, x, y, y_next, v, d, cost, holding, load, plants,
    x1, inner, outer, loads, prices,
):
    primal = step_size(codes, 0)
    rows = row_ids()
    plant_ids = lax.broadcasted_iota(jnp.int32, (P_SIZE, BLOCK), 0)
    odd = codes[2] == 1
    width = x.shape[1]
    each = P_SIZE // gathered.shape[0]
    for j in range(gathered.shape[0]):
        prices[:, j * each : (j + 1) * each] = gathered[j, 0:ROWS, 0:each]
    w = prices[...]
    total = jnp.zeros((P_SIZE, 3 * ROWS), F32)
    for i, at in blocks(width):
        lag = lags[i]
        yb = y_next[:, at]
        dual = ahead(y[:, at], yb, lag, rows)
        old = x[:, at]
        charged = price_of(w, plants[:, at]) * load[:, at]
        new = jnp.maximum(old - primal * (cost[:, at] + dual + charged), 0.0)
        over = 2.0 * new - old
        x1[:, at] = new
        total += load_terms(over * load[:, at], plants[:, at], plant_ids)
        v7 = v[7:8, at]
        bar7 = 2.0 * stock_step(v7, holding[:, at], y[7:8, at], yb[0:1], primal) - v7
        field8 = y_next[extra_slot(i, width, 0)] + bar7
        first_row = over[0:1] + jnp.where(lag == LAGMAX, field8, 0.0)
        down = jnp.where(rows == 0, first_row, jnp.where(rows == 1, yb[0:1], d[:, at]))
        up = over + jnp.where(rows == ROWS - lag, bar7, 0.0)
        inner[:, at] = jnp.where(odd, down, up)
        outer[:, at] = jnp.where(odd, up, down)
    loads[...] = jnp.broadcast_to(folded(total)[None], loads.shape)


def middle_kernel(
    codes, lags, x, x1, inner, outer, y, y_next, v, v_next, d, holding,
    v2, dual_x, field_x,
):
    primal = step_size(codes, 0)
    dual_step = step_size(codes, 1)
    rows = row_ids()
    odd = codes[2] == 1
    width = v.shape[1]
    square = jnp.zeros((ROWS, BLOCK), F32)
    for i, at in blocks(width):
        lag = lags[i]
        cost = holding[:, at]
        ya, yb = y[:, at], y_next[:, at]
        va, vb = v[:, at], v_next[:, at]
        pair = inner[:, at], outer[:, at]
        bar_prev, mixed = jnp.where(odd, *pair), jnp.where(odd, *pair[::-1])
        da = d[:, at]
        d8, d9 = v_next[extra_slot(i, width, 0)], v_next[extra_slot(i, width, 1)]
        bar8, y16 = mixed[0:1], mixed[1:2]
        db = jnp.where(rows == 0, d8, jnp.where(rows == 1, d9, mixed))
        over = 2.0 * x1[:, at] - x[:, at]
        va1 = stock_step(va, cost, ya, row_after(ya, yb[0:1], rows), primal)
        vb1 = stock_step(vb, cost, yb, row_after(yb, y16, rows), primal)
        va_bar = 2.0 * va1 - va
        vb_bar = 2.0 * vb1 - vb
        ha = -da - va_bar + row_before(va_bar, jnp.zeros((1, BLOCK), F32), rows)
        hb = -db - vb_bar + row_before(vb_bar, va_bar[7:8], rows)
        misfit = ahead(ha, hb, lag, rows) + over
        square += misfit * misfit
        yx = ahead(ya, yb, lag, rows) + dual_step * misfit
        dual_x[:, at] = yx
        ya1 = ya + dual_step * (ha + past(over, bar_prev, lag, rows))
        y8 = yb[0:1] + dual_step * (hb[0:1] + pltpu.roll(over, lag & (ROWS - 1), 0)[0:1])
        va2 = stock_step(va1, cost, ya1, row_after(ya1, y8, rows), primal)
        v2[:, at] = va2
        start_bar = pltpu.roll(2.0 * va2 - va1, (ROWS - lag + 1) & (ROWS - 1), 0)[0:1]
        whole = lag == LAGMAX
        y_end = jnp.where(whole, y16, pltpu.roll(yb, ROWS - lag, 0)[0:1])
        h_end = jnp.where(whole, 0.0, pltpu.roll(hb, ROWS - lag, 0)[0:1])
        yx_end = y_end + dual_step * (h_end + bar8)
        vx1 = ahead(va1, vb1, lag, rows)
        vx2 = stock_step(vx1, cost, yx, row_after(yx, yx_end, rows), primal)
        vx_bar = 2.0 * vx2 - vx1
        dx = ahead(da, db, lag, rows)
        field_x[:, at] = -dx - vx_bar + row_before(vx_bar, start_bar, rows)
    field_x[:, width : width + BLOCK] = square


def second_kernel(
    codes, sums, prices, cap, x, dual, field, cost, load, plants,
    x2, dual_x, loads, prices_new, excess_row,
):
    primal = step_size(codes, 0)
    dual_step = step_size(codes, 1)
    plant_step = dual_step * (P_SIZE / (x.shape[1] * sums.shape[0]))
    plant_ids = lax.broadcasted_iota(jnp.int32, (P_SIZE, BLOCK), 0)
    excess = jnp.sum(sums[...], axis=0) - cap[...]
    w = jnp.maximum(prices[...] + plant_step * excess, 0.0)
    prices_new[...] = w
    above = jnp.maximum(excess, 0.0)
    excess_row[...] = jnp.sum(above * above, axis=0, keepdims=True)
    total = jnp.zeros((P_SIZE, 3 * ROWS), F32)
    square = jnp.zeros((ROWS, BLOCK), F32)
    for i, at in blocks(x.shape[1]):
        old = x[:, at]
        charged = price_of(w, plants[:, at]) * load[:, at]
        new = jnp.maximum(old - primal * (cost[:, at] + dual[:, at] + charged), 0.0)
        over = 2.0 * new - old
        x2[:, at] = new
        misfit = field[:, at] + over
        dual_x[:, at] = dual[:, at] + dual_step * misfit
        square += misfit * misfit
        total += load_terms(over * load[:, at], plants[:, at], plant_ids)
    own = folded(total)
    pair = (field[:, x.shape[1] :], square)
    lines = [own[k : k + 1] for k in range(ROWS)]
    lines += [jnp.sum(p, axis=0, keepdims=True) for p in pair]
    for k, line in enumerate(lines):
        at = slice(k * P_SIZE, (k + 1) * P_SIZE)
        loads[:, :, at] = jnp.broadcast_to(line[None], (loads.shape[0], 1, P_SIZE))


def third_kernel(codes, sums, prices, cap, excess_row, price_out, out, *, total_skus, total_rows):
    plant_step = step_size(codes, 1) * (P_SIZE / total_skus)
    row = jnp.sum(sums[...], axis=0)
    totals = jnp.concatenate(
        [row[:, k * P_SIZE : (k + 1) * P_SIZE] for k in range(ROWS + 2)], axis=0
    )
    excess = totals[0:8] - cap[...]
    price_out[...] = jnp.maximum(prices[...] + plant_step * excess, 0.0)
    above = jnp.maximum(excess, 0.0)
    above_row = jnp.sum(above * above, axis=0, keepdims=True)
    for k, rows in enumerate(((totals[8:9], excess_row[...]), (totals[9:10], above_row))):
        cells, scale = total_rows * total_skus, P_SIZE / total_skus
        pair = jnp.concatenate(
            [rows[0] * (1.0 / cells), rows[1] * (scale * scale / (total_rows * P_SIZE))], 0
        )
        out[:, k] = jnp.broadcast_to(pair[None], (out.shape[0],) + pair.shape)


def unshift_kernel(lags, dual, dual_prev, y):
    rows = row_ids()
    for i, at in blocks(y.shape[1]):
        y[:, at] = past(dual[:, at], dual_prev[:, at], lags[i], rows)


def body(
    primal_x,
    stock_v,
    balance_dual,
    plant_dual,
    demand,
    unit_cost,
    holding_cost,
    load_coef,
    capacity,
    lags,
    plants,
    step_codes,
):
    width = primal_x.shape[1]
    skus = lax.axis_size("sku")
    times = lax.axis_size("tm")
    each = plant_dual.shape[1]
    total_skus = width * skus
    owner = lax.axis_index("sku") * each
    cost = unit_cost.reshape(1, width)
    holding = holding_cost.reshape(1, width)
    load = load_coef.reshape(1, width)
    plant_row = plants.reshape(1, width)

    payload, y_sent = start(
        step_codes, plant_dual, balance_dual, stock_v, demand, holding, skus
    )
    y_next = shifted(y_sent, "tm", -1)
    payload, codes, lags, v, d, *held = lax.optimization_barrier(
        (
            payload, step_codes, lags, stock_v, demand, primal_x, balance_dual, cost, holding,
            load, plant_row, capacity,
        )
    )
    codes, lags, v, d, x, y, cost, holding, load, plant_row, limits, v_sent = stage(
        (codes, lags), v, d, held
    )
    v_next = shifted(v_sent, "tm", -1)
    gathered = spread(payload, "sku")
    x1, inner, outer, loads1, prices0 = call(
        first_kernel,
        (
            near(ROWS, width), near(ROWS, width), near(ROWS, width),
            shape(skus, ROWS, P_SIZE), near(ROWS, P_SIZE),
        ),
        (codes, lags, gathered, x, y, y_next, v, d, cost, holding, load, plant_row),
        smem=2,
        name="first",
    )
    inner = swapped(inner, "tm", 0)
    outer = swapped(outer, "tm", 1)
    sums1 = spread(loads1, "sku")
    v2, dual_x, field_x = call(
        middle_kernel,
        (near(ROWS, width), near(ROWS, width), near(ROWS, width + BLOCK)),
        (codes, lags, x, x1, inner, outer, y, y_next, v, v_next, d, holding),
        smem=2,
        name="middle",
    )
    x2, dual_x2, loads2, prices1, above1 = call(
        second_kernel,
        (
            near(ROWS, width), near(ROWS, width), shape(skus, 1, (ROWS + 2) * P_SIZE),
            near(ROWS, P_SIZE), near(1, P_SIZE),
        ),
        (
            codes, sums1, prices0, limits, x1, dual_x, field_x, cost, load,
            plant_row,
        ),
        smem=1,
        name="second",
    )
    sums2 = spread(loads2, "sku")
    dual_prev = shifted(dual_x2, "tm", 1)

    def third(*refs):
        third_kernel(*refs, total_skus=total_skus, total_rows=ROWS * times)

    prices2, packed = call(
        third,
        (near(ROWS, P_SIZE), shape(times, 2, 2, P_SIZE)),
        (codes, sums2, prices1, limits, above1),
        smem=1,
        name="third",
    )
    portion = lax.dynamic_slice_in_dim(prices2, owner, each, 1)
    residuals = jnp.sum(spread_rows(packed), axis=(0, 3))
    next_y = call(
        unshift_kernel, shape(ROWS, width), (lags, dual_x2, dual_prev), smem=1, name="unshift"
    )
    return x2, v2, next_y, portion, residuals


def solution(mesh):
    return jax.shard_map(
        body,
        mesh=mesh,
        in_specs=(
            P("tm", "sku"),
            P("tm", "sku"),
            P("tm", "sku"),
            P("tm", "sku"),
            P("tm", "sku"),
            P("sku"),
            P("sku"),
            P("sku"),
            P("tm", None),
            P("sku"),
            P("sku"),
            P(),
        ),
        out_specs=(P("tm", "sku"), P("tm", "sku"), P("tm", "sku"), P("tm", "sku"), P()),
        check_vma=False,
    )
```
